32 devices in a mesh: span: 4 (over y, x), plane: 8 (over z, core).
Axes of the slice: x: 2, y: 2, z: 4, core: 2. Of those that a mesh axis runs over, the one named last changes fastest.
Arguments:
- state: float32 [512, 40, 640], P('span', 'plane'), may hold values from -8 to 8, as said below
- wall_tag: int32 [128], replicated, may hold values 0 or 1
Outputs:
- new_state: float32 [512, 40, 640], P('span', 'plane')
The draws below stay inside these ranges and needn't reach their ends.
Inputs may be any that keep to these rules, and one draw needn't show every extreme that they name: `state`: spectral coefficients of the conserved variable.
All inputs are finite; a program needn't handle non-finite values.
Results may differ from the reference program's by a relative error of at most 0.0001.
Values sent between devices are 32-bit elements; how exact they have to be, the bound alone decides.
A program may use at most 64 MiB of HBM per device.

```python
import math
import jax
import jax.numpy as jnp
import numpy as np
from jax import lax

KMODES = 256
MODES = 512
PLANES = 768
GX = 128
ITERS = 3
ROWS = 40
COLS = 640


def draw_state(key, part):
    values = jnp.clip(jax.random.normal(key, (MODES, ROWS, COLS), jnp.float32), -4.0, 4.0)
    height = jnp.arange(ROWS, dtype=jnp.float32) / (ROWS - 1)
    profile = 0.6 * jnp.exp(height * math.log(3.0))
    return values * profile[None, :, None]


def set_ends(drawn, rng, smallest, largest):
    index_at = [jax.random.randint(jax.random.fold_in(rng, axis), (), 0, length) for axis, length in enumerate(drawn.shape)]
    longest = drawn.shape.index(max(drawn.shape))
    next_to = index_at[:longest] + [(index_at[longest] + 1) % drawn.shape[longest]] + index_at[longest + 1:]
    return drawn.at[tuple(index_at)].set(smallest).at[tuple(next_to)].set(largest)


def setup_inputs(seed: int = 0) -> dict:
    keys = jax.random.split(jax.random.key(seed), 3)
    return {
        "state": draw_state(jax.random.fold_in(keys[2], 71), 0),
        "wall_tag": set_ends((jax.random.randint(keys[1], (GX,), 0, 2) < 1).astype(jnp.int32), jax.random.fold_in(keys[1], 1), 0, 1),
    }


highest = lax.Precision.HIGHEST
step_size = 0.03
viscous = 0.05
span_stiff = 4.0

def gll_tables():
    abscissae = np.array([-1.0, -math.sqrt(3.0 / 7.0), 0.0, math.sqrt(3.0 / 7.0), 1.0])
    weights = np.array([0.1, 49.0 / 90.0, 32.0 / 45.0, 49.0 / 90.0, 0.1])
    squared = abscissae * abscissae
    legendre = (35.0 * squared * squared - 30.0 * squared + 3.0) / 8.0
    identity = np.eye(5)
    spacing = abscissae[:, None] - abscissae[None, :] + identity
    differ = np.where(identity > 0, 0.0, legendre[:, None] / legendre[None, :] / spacing)
    differ[0, 0] = -5.0
    differ[4, 4] = 5.0
    stiffness = differ.T @ (weights[:, None] * differ)
    return (jnp.asarray(differ, dtype=jnp.float32), jnp.asarray(weights, dtype=jnp.float32), jnp.asarray(stiffness, dtype=jnp.float32))

def inverse_basis(plane_ids, kmodes, planes):
    wavenumber = jnp.arange(kmodes, dtype=jnp.int32)
    phase_index = plane_ids[:, None] * wavenumber[None, :] % planes
    angles = phase_index.astype(jnp.float32) * (2.0 * math.pi / planes)
    basis = jnp.stack([jnp.cos(angles), jnp.sin(angles)], axis=2).reshape(plane_ids.shape[0], 2 * kmodes)
    return basis / math.sqrt(kmodes)

def forward_basis(kmodes, planes):
    wavenumber = jnp.arange(kmodes, dtype=jnp.int32)
    plane_ids = jnp.arange(planes, dtype=jnp.int32)
    phase_index = wavenumber[:, None] * plane_ids[None, :] % planes
    angles = phase_index.astype(jnp.float32) * (2.0 * math.pi / planes)
    factor = jnp.where(wavenumber == 0, 1.0, 2.0).astype(jnp.float32) * (math.sqrt(kmodes) / planes)
    basis = jnp.stack([jnp.cos(angles) * factor[:, None], jnp.sin(angles) * factor[:, None]], axis=1)
    return basis.reshape(2 * kmodes, planes)

def combine_spectra(inner_part, span_part, kmodes):
    shape = inner_part.shape
    inner_pair = inner_part.reshape((kmodes, 2) + shape[1:])
    span_pair = span_part.reshape((kmodes, 2) + shape[1:])
    ratio = (jnp.arange(kmodes, dtype=jnp.float32) / kmodes)[:, None, None]
    cos_part = inner_pair[:, 0] - ratio * span_pair[:, 1]
    sin_part = inner_pair[:, 1] + ratio * span_pair[:, 0]
    return jnp.stack([cos_part, sin_part], axis=1).reshape(shape)

def two_point(left_state, right_state):
    mean_part = (left_state * left_state + left_state * right_state + right_state * right_state) / 6.0
    speed = jnp.maximum(jnp.abs(left_state), jnp.abs(right_state))
    return mean_part - 0.5 * speed * (right_state - left_state)

def split_form(physical, below_row, above_row, differ):
    planes, row_count, col_count = physical.shape
    square = physical * physical
    slope_x = jnp.einsum('ai,prxi->prxa', differ, physical.reshape(planes, row_count, col_count // 5, 5), precision=highest).reshape(planes, row_count, col_count)
    square_x = jnp.einsum('ai,prxi->prxa', differ, square.reshape(planes, row_count, col_count // 5, 5), precision=highest).reshape(planes, row_count, col_count)
    slope_y = jnp.einsum('aj,pejc->peac', differ, physical.reshape(planes, row_count // 5, 5, col_count), precision=highest).reshape(planes, row_count, col_count)
    square_y = jnp.einsum('aj,pejc->peac', differ, square.reshape(planes, row_count // 5, 5, col_count), precision=highest).reshape(planes, row_count, col_count)
    volume = (square_x + physical * slope_x + square_y + physical * slope_y) / 3.0
    half_square = 0.5 * square
    col_node = (jnp.arange(col_count) % 5)[None, None, :]
    row_node = (jnp.arange(row_count) % 5)[:, None]
    left_side = jnp.roll(physical, 1, axis=2)
    right_side = jnp.roll(physical, -1, axis=2)
    surface_rhs = -volume
    surface_rhs = surface_rhs + jnp.where(col_node == 0, 10.0 * (two_point(left_side, physical) - half_square), 0.0)
    surface_rhs = surface_rhs - jnp.where(col_node == 4, 10.0 * (two_point(physical, right_side) - half_square), 0.0)
    surface_rhs = surface_rhs + jnp.where(row_node == 0, 10.0 * (two_point(below_row, physical) - half_square), 0.0)
    surface_rhs = surface_rhs - jnp.where(row_node == 4, 10.0 * (two_point(physical, above_row) - half_square), 0.0)
    return (surface_rhs, half_square)

def join_columns(values):
    mode_count, row_count, col_count = values.shape
    blocks = values.reshape(mode_count, row_count, col_count // 5, 5)
    pair_sum = blocks[..., 4] + jnp.roll(blocks[..., 0], -1, axis=2)
    blocks = jnp.concatenate([jnp.roll(pair_sum, 1, axis=2)[..., None], blocks[..., 1:4], pair_sum[..., None]], axis=3)
    return blocks.reshape(mode_count, row_count, col_count)

def join_rows(joined, below_row, above_row):
    row_node = (jnp.arange(joined.shape[1]) % 5)[:, None]
    return joined + jnp.where(row_node == 0, below_row, 0.0) + jnp.where(row_node == 4, above_row, 0.0)

def assemble_whole(values):
    joined = join_columns(values)
    zero_row = jnp.zeros_like(joined[:, :1])
    below_row = jnp.concatenate([zero_row, joined[:, :-1]], axis=1)
    above_row = jnp.concatenate([joined[:, 1:], zero_row], axis=1)
    return join_rows(joined, below_row, above_row)

def local_helmholtz(values, shift_coeff, row_weight, col_weight, stiffness):
    mode_count, row_count, col_count = values.shape
    stiff_x = jnp.einsum('ai,mrxi->mrxa', stiffness, values.reshape(mode_count, row_count, col_count // 5, 5), precision=highest).reshape(mode_count, row_count, col_count)
    stiff_y = jnp.einsum('aj,mejc->meac', stiffness, values.reshape(mode_count, row_count // 5, 5, col_count), precision=highest).reshape(mode_count, row_count, col_count)
    mass_diag = row_weight[:, None] * col_weight[None, :]
    return shift_coeff * mass_diag * values + viscous * (row_weight[:, None] * stiff_x + col_weight[None, :] * stiff_y)

def weighted_dot(first_vec, second_vec, inv_mult):
    return lax.optimization_barrier(jnp.sum(first_vec * second_vec * inv_mult, axis=(1, 2)))

def reference(state, wall_tag):
    differ, weights, stiffness = gll_tables()
    mode_count, row_count, col_count = state.shape
    inverse = inverse_basis(jnp.arange(PLANES, dtype=jnp.int32), KMODES, PLANES)
    physical = jnp.einsum('pm,mrc->prc', inverse, state, precision=highest)
    tag_cols = jnp.repeat(wall_tag, 5)[None, :]
    mirror = jnp.where(tag_cols == 1, -physical[:, 0, :], physical[:, 0, :])
    below_row = jnp.concatenate([mirror[:, None, :], physical[:, :-1]], axis=1)
    above_row = jnp.concatenate([physical[:, 1:], physical[:, -1:]], axis=1)
    surface_rhs, half_square = split_form(physical, below_row, above_row, differ)
    forward = forward_basis(KMODES, PLANES)
    inner_part = jnp.einsum('mp,prc->mrc', forward, surface_rhs, precision=highest)
    span_part = jnp.einsum('mp,prc->mrc', forward, half_square, precision=highest)
    tendency = combine_spectra(inner_part, span_part, KMODES)
    predicted = state + step_size * tendency
    wavenumber = (jnp.arange(mode_count, dtype=jnp.int32) // 2).astype(jnp.float32) / KMODES
    shift_coeff = (1.0 + span_stiff * wavenumber * wavenumber)[:, None, None]
    row_weight = jnp.tile(weights, row_count // 5)
    col_weight = jnp.tile(weights, col_count // 5)
    row_node = jnp.arange(row_count) % 5
    row_ids = jnp.arange(row_count)
    row_half = jnp.where(((row_node == 0) | (row_node == 4)) & (row_ids != 0) & (row_ids != row_count - 1), 0.5, 1.0)
    col_node = jnp.arange(col_count) % 5
    col_half = jnp.where((col_node == 0) | (col_node == 4), 0.5, 1.0)
    inv_mult = (row_half[:, None] * col_half[None, :]).astype(jnp.float32)
    load_vec = assemble_whole(row_weight[:, None] * col_weight[None, :] * predicted)
    solution = jnp.zeros_like(load_vec)
    residual = load_vec
    direction = load_vec
    norm_now = weighted_dot(residual, residual, inv_mult)
    for iteration in range(ITERS):
        applied = assemble_whole(local_helmholtz(direction, shift_coeff, row_weight, col_weight, stiffness))
        step_len = (norm_now / weighted_dot(direction, applied, inv_mult))[:, None, None]
        solution = solution + step_len * direction
        residual = residual - step_len * applied
        norm_next = weighted_dot(residual, residual, inv_mult)
        direction = residual + (norm_next / norm_now)[:, None, None] * direction
        norm_now = norm_next
    return solution
```

```python
import functools
import math

import jax
import jax.numpy as jnp
import numpy as np
from jax import lax
from jax.experimental import pallas as pl
from jax.experimental.pallas import tpu as pltpu
from jax.sharding import PartitionSpec as P

KMODES = 256
PLANES = 768
STEP = 0.03
VISCOUS = 0.05
STIFF = 4.0
PAD = 16

f32 = jnp.float32
bf16 = jnp.bfloat16
NT = (((1,), (1,)), ((), ()))
NN = (((1,), (0,)), ((), ()))
TN = (((0,), (0,)), ((), ()))
VMEM_LIMIT = 56 * 1024 * 1024


def gll_tables():
    x = np.array([-1.0, -math.sqrt(3.0 / 7.0), 0.0, math.sqrt(3.0 / 7.0), 1.0])
    w = np.array([0.1, 49.0 / 90.0, 32.0 / 45.0, 49.0 / 90.0, 0.1])
    q = x * x
    leg = (35.0 * q * q - 30.0 * q + 3.0) / 8.0
    eye = np.eye(5)
    d = np.where(eye > 0, 0.0, leg[:, None] / leg[None, :] / (x[:, None] - x[None, :] + eye))
    d[0, 0], d[4, 4] = -5.0, 5.0
    return d, w, d.T @ (w[:, None] * d)


DIFF, WEIGHT, KMAT = gll_tables()


def halves(table):
    high = table.astype(np.float32).astype(bf16)
    low = (table.astype(np.float32) - high.astype(np.float32)).astype(bf16)
    return high, low


def basis_tables():
    k, p = np.arange(KMODES), np.arange(PLANES)
    angle = 2.0 * math.pi * (p[:, None] * k[None, :] % PLANES) / PLANES
    cos, sin = np.cos(angle), np.sin(angle)
    inverse = np.stack([cos, sin], 2).reshape(PLANES, 2 * KMODES).T / math.sqrt(KMODES)
    factor = np.where(k == 0, 1.0, 2.0) * (math.sqrt(KMODES) / PLANES) * STEP
    ratio = k / KMODES
    inner = np.stack([cos * factor, sin * factor], 2).reshape(PLANES, 2 * KMODES)
    span = np.stack([-ratio * sin * factor, ratio * cos * factor], 2).reshape(PLANES, 2 * KMODES)
    return inverse, inner, span


def split2(x):
    high = x.astype(bf16)
    return high, (x - high.astype(f32)).astype(bf16)


def split3(x):
    high = x.astype(bf16)
    rest = x - high.astype(f32)
    mid = rest.astype(bf16)
    return high, mid, (rest - mid.astype(f32)).astype(bf16)


def dot(a, b, dims=NN):
    return lax.dot_general(a, b, dims, preferred_element_type=f32)


def along(mat, a, flip):
    s1, d1, s2, d2, m = a[0] + a[4], a[0] - a[4], a[1] + a[3], a[1] - a[3], a[2]
    out = [None] * 5
    for r in (0, 1):
        e = [0.5 * (mat[r][b] + mat[r][4 - b]) for b in (0, 1)]
        o = [0.5 * (mat[r][b] - mat[r][4 - b]) for b in (0, 1)]
        even = float(e[0]) * s1 + float(e[1]) * s2 + float(mat[r][2]) * m
        odd = float(o[0]) * d1 + float(o[1]) * d2
        out[r] = even + odd
        out[4 - r] = even - odd if flip > 0 else odd - even
    if flip > 0:
        out[2] = float(mat[2][0]) * s1 + float(mat[2][1]) * s2 + float(mat[2][2]) * m
    else:
        out[2] = float(mat[2][0]) * d1 + float(mat[2][1]) * d2
    return out


def two_point10(a, b, qa, qb):
    speed = jnp.maximum(jnp.abs(a), jnp.abs(b))
    return (qa + a * b + qb) * (10.0 / 6.0) - 5.0 * speed * (b - a)


def roll(x, by):
    return pltpu.roll(x, by % x.shape[0], 0)


def pack(x_ref, perm_ref, d_ref, span, elems):
    modes, rows, cols = x_ref.shape
    block = 5 * elems
    x = jnp.concatenate([x_ref[:, j, :] for j in range(rows)], axis=0)
    parts = split3(x)
    for s in range(span):
        lo = block * s // 128 * 128
        hi = -(-block * (s + 1) // 128) * 128
        perm = perm_ref[s, :, : hi - lo]
        got = sum(dot(perm, part[:, lo:hi], NT) for part in parts)
        for j in range(rows):
            d_ref[s, block * j : block * (j + 1), :] = got[:, modes * j : modes * (j + 1)]
    for s in range(span):
        left, right = (s - 1) % span, (s + 1) % span
        for j in range(rows):
            at = block * rows + 2 * j
            last = block * j + block - 1
            d_ref[s, at : at + 1, :] = d_ref[left, last : last + 1, :]
            d_ref[s, at + 1 : at + 2, :] = d_ref[right, block * j : block * j + 1, :]
        for at in range(block * rows + 2 * rows, block * rows + PAD):
            d_ref[s, at : at + 1, :] = jnp.zeros((1, modes), f32)


def perm_tables(span, elems):
    block = 5 * elems
    width = max(-(-block * (s + 1) // 128) * 128 - block * s // 128 * 128 for s in range(span))
    perm = np.zeros((span, block, width), np.float32)
    for s in range(span):
        lo = block * s // 128 * 128
        for i in range(5):
            for e in range(elems):
                perm[s, i * elems + e, block * s + 5 * e + i - lo] = 1.0
    return perm.astype(bf16)


def physical(recv_ref, below_ref, above_ref, tag_ref, inv_ref, fld_ref, elems, first, last):
    span, sr, modes = recv_ref.shape
    block = 5 * elems
    x = jnp.concatenate(
        [
            jnp.concatenate([ref[s] for s in range(span)], axis=1)
            for ref in (recv_ref, below_ref, above_ref)
        ],
        axis=0,
    )
    high, low = split2(x)
    step = 256
    for n in range(PLANES // step):
        at = slice(n * step, (n + 1) * step)
        bh, bl = inv_ref[0, :, at], inv_ref[1, :, at]
        fld_ref[:, at] = dot(high, bh) + dot(high, bl) + dot(low, bh)
    own0 = fld_ref[0:block, :]
    mirror = jnp.where(tag_ref[...] == 1, -own0, own0)
    fld_ref[sr : sr + block, :] = jnp.where(first, mirror, fld_ref[sr : sr + block, :])
    own4 = fld_ref[4 * block : 5 * block, :]
    fld_ref[sr + block : sr + 2 * block, :] = jnp.where(
        last, own4, fld_ref[sr + block : sr + 2 * block, :]
    )


def pointwise(fld_ref, r_ref, h_ref, elems):
    block = 5 * elems
    sr = 5 * block + PAD
    lane = 128
    third = DIFF * (-1.0 / 3.0)

    def body(n, _):
        at = pl.ds(pl.multiple_of(n * lane, lane), lane)
        row = lax.broadcasted_iota(jnp.int32, (elems, lane), 0)

        def load(k):
            return fld_ref[k : k + elems, at]

        u = [[load(block * j + elems * i) for i in range(5)] for j in range(5)]
        q = [[v * v for v in r] for r in u]
        rhs = [[None] * 5 for _ in range(5)]
        for j in range(5):
            du = along(third, u[j], -1)
            dq = along(third, q[j], -1)
            for i in range(5):
                rhs[j][i] = dq[i] + u[j][i] * du[i]
            hl = fld_ref[5 * block + 2 * j : 5 * block + 2 * j + 1, at]
            hr = fld_ref[5 * block + 2 * j + 1 : 5 * block + 2 * j + 2, at]
            left = jnp.where(row == 0, hl, roll(u[j][4], 1))
            right = jnp.where(row == elems - 1, hr, roll(u[j][0], -1))
            rhs[j][0] += two_point10(left, u[j][0], left * left, q[j][0]) - 5.0 * q[j][0]
            rhs[j][4] -= two_point10(u[j][4], right, q[j][4], right * right) - 5.0 * q[j][4]
        for i in range(5):
            ui, qi = [u[j][i] for j in range(5)], [q[j][i] for j in range(5)]
            du = along(third, ui, -1)
            dq = along(third, qi, -1)
            for j in range(5):
                rhs[j][i] += dq[j] + ui[j] * du[j]
            lower = load(sr + elems * i)
            upper = load(sr + block + elems * i)
            rhs[0][i] += two_point10(lower, ui[0], lower * lower, qi[0]) - 5.0 * qi[0]
            rhs[4][i] -= two_point10(ui[4], upper, qi[4], upper * upper) - 5.0 * qi[4]
        for ref, val, scale in ((r_ref, rhs, None), (h_ref, q, 0.5)):
            for j in range(5):
                a = val[j] if scale is None else [scale * v for v in val[j]]
                ref[4 * elems * j : 4 * elems * j + elems, at] = a[0] + jnp.where(
                    row == 0, 0.0, roll(a[4], 1)
                )
                for i in (1, 2, 3):
                    k = elems * (4 * j + i)
                    ref[k : k + elems, at] = a[i]
                ref[20 * elems + j : 20 * elems + j + 1, at] = a[4][elems - 1 : elems, :]
            ref[20 * elems + 5 : 20 * elems + PAD, at] = jnp.zeros((PAD - 5, lane), f32)
        return 0

    lax.fori_loop(0, PLANES // lane, body, 0)


def spectral(r_ref, h_ref, fwd_ref, t_ref):
    span, _, modes = t_ref.shape
    rh, rl = split2(r_ref[...])
    hh, hl = split2(h_ref[...])
    step = max(modes, 256)
    for n in range(span * modes // step):
        at = slice(n * step, (n + 1) * step)
        a, b = fwd_ref[0, :, at], fwd_ref[1, :, at]
        c, d = fwd_ref[2, :, at], fwd_ref[3, :, at]
        t = dot(rh, a) + dot(rl, a) + dot(rh, b) + dot(hh, c) + dot(hl, c) + dot(hh, d)
        for k in range(step // modes):
            t_ref[n * (step // modes) + k] = t[:, modes * k : modes * (k + 1)]


def column_load(d_ref, t_ref, c_ref, elems):
    span, _, modes = d_ref.shape
    block = 5 * elems
    total = span * elems
    row = lax.broadcasted_iota(jnp.int32, (elems, modes), 0)
    for j in range(5):
        for s in range(span):
            left = (s - 1) % span
            for i in range(4):
                k = block * j + elems * i
                val = d_ref[s, k : k + elems, :] + t_ref[s, elems * (4 * j + i) : elems * (4 * j + i + 1), :]
                if i == 0:
                    k4 = block * j + 4 * elems
                    extra = 20 * elems + j
                    edge = d_ref[left, k4 + elems - 1 : k4 + elems, :] + t_ref[left, extra : extra + 1, :]
                    val += jnp.where(row == 0, edge, roll(d_ref[s, k4 : k4 + elems, :], 1))
                c_ref[j, i, elems * s : elems * (s + 1), :] = val * float(WEIGHT[j] * WEIGHT[i])


def apply_local(v_ref, out_ref, shift):
    col = [2.0 * WEIGHT[0], WEIGHT[1], WEIGHT[2], WEIGHT[3]]
    for j in range(5):
        a = [v_ref[j, i] for i in range(4)]
        a.append(roll(a[0], -1))
        kx = along(KMAT * (VISCOUS * WEIGHT[j]), a, 1)
        kx[0] = kx[0] + roll(kx[4], 1)
        for i in range(4):
            out_ref[j, i] = kx[i]
    total = 0.0
    for i in range(4):
        a = [v_ref[j, i] for j in range(5)]
        ky = along(KMAT * (VISCOUS * col[i]), a, 1)
        for j in range(5):
            val = out_ref[j, i] + ky[j] + (shift * float(WEIGHT[j] * col[i])) * a[j]
            out_ref[j, i] = val
            total = total + jnp.sum(val * a[j], axis=0, keepdims=True)
    return total


def square_sum(v_ref, first, last):
    total = 0.0
    for j in range(5):
        part = sum(jnp.sum(v_ref[j, i] * v_ref[j, i], axis=0, keepdims=True) for i in range(4))
        if j == 0:
            part = part * jnp.where(first, 1.0, 0.5)
        if j == 4:
            part = part * jnp.where(last, 1.0, 0.5)
        total = total + part
    return total


def solve3(nu, theta):
    a = [[nu[r + c + 1] + theta * nu[r + c] for c in range(3)] for r in range(3)]
    l10, l20 = a[1][0] / a[0][0], a[2][0] / a[0][0]
    d1 = a[1][1] - l10 * a[1][0]
    e = a[2][1] - l20 * a[1][0]
    l21 = e / d1
    d2 = a[2][2] - l20 * a[2][0] - l21 * e
    z0 = nu[0]
    z1 = nu[1] - l10 * z0
    z2 = nu[2] - l20 * z0 - l21 * z1
    y2 = z2 / d2
    y1 = z1 / d1 - l21 * y2
    return z0 / a[0][0] - l10 * y1 - l20 * y2, y1, y2


def unpack(v0_ref, v1_ref, v2_ref, y_ref, exp_ref, out_ref):
    elems, modes = v0_ref.shape[2:]
    y = [y_ref[k : k + 1, :] for k in range(3)]
    for j in range(5):
        x = jnp.concatenate(
            [y[0] * v0_ref[j, i] + y[1] * v1_ref[j, i] + y[2] * v2_ref[j, i] for i in range(4)], axis=0
        )
        out_ref[:, j, :] = sum(dot(part, exp_ref[...], TN) for part in split2(x))


def expand_table(total):
    out = np.zeros((4 * total, 5 * total), np.float32)
    for e in range(total):
        for i in range(5):
            out[(i % 4) * total + (e + i // 4) % total, 5 * e + i] = 1.0
    return out.astype(bf16)


def call(body, outs, scratch=(), **kw):
    return pl.pallas_call(
        body,
        out_shape=outs,
        scratch_shapes=list(scratch),
        compiler_params=pltpu.CompilerParams(vmem_limit_bytes=VMEM_LIMIT),
        **kw,
    )


def shape(*dims):
    return jax.ShapeDtypeStruct(dims, f32)


def on_device(state, wall_tag):
    modes, rows, cols = state.shape
    assert rows == 5
    span, planes = lax.axis_size("span"), lax.axis_size("plane")
    total = cols // 5
    elems = total // span
    block = 5 * elems
    sr, tr = 5 * block + PAD, 20 * elems + PAD
    my_span, my_plane = lax.axis_index("span"), lax.axis_index("plane")
    first, last = my_plane == 0, my_plane == planes - 1
    up = [(i, i + 1) for i in range(planes - 1)]
    down = [(i + 1, i) for i in range(planes - 1)]

    inverse, inner, outer = basis_tables()
    inv = jnp.asarray(np.stack(halves(inverse)))
    fwd = jnp.asarray(np.stack(halves(inner) + halves(outer)))
    perm = jnp.asarray(perm_tables(span, elems))
    expand = jnp.asarray(expand_table(total))
    ids = my_span * modes + jnp.arange(modes, dtype=jnp.int32)
    wave = (ids // 2).astype(f32) / KMODES
    shift = (1.0 + STIFF * wave * wave)[None, :]
    theta = 0.6 + 0.254 * (shift - 1.0)
    tags = jnp.tile(lax.dynamic_slice_in_dim(wall_tag, my_span * elems, elems, 0), 5)[:, None]
    edge = jnp.stack([first, last]).astype(jnp.int32)
    smem = pl.BlockSpec(memory_space=pltpu.SMEM)
    vmem = pl.BlockSpec(memory_space=pltpu.VMEM)

    own = call(lambda x, p, d: pack(x, p, d, span, elems), shape(span, sr, modes))(state, perm)
    recv = lax.all_to_all(own, "span", 0, 0, tiled=True)
    below = lax.ppermute(recv[:, 4 * block : 5 * block], "plane", up)
    above = lax.ppermute(recv[:, :block], "plane", down)

    def middle(edge_ref, x, lo, hi, tag, inv_ref, fwd_ref, t_ref, fld, r, h):
        physical(x, lo, hi, tag, inv_ref, fld, elems, edge_ref[0] == 1, edge_ref[1] == 1)
        pointwise(fld, r, h, elems)
        spectral(r, h, fwd_ref, t_ref)

    sent = call(
        middle,
        shape(span, tr, modes),
        [
            pltpu.VMEM((sr + 2 * block, PLANES), f32),
            pltpu.VMEM((tr, PLANES), f32),
            pltpu.VMEM((tr, PLANES), f32),
        ],
        in_specs=[smem] + [vmem] * 6,
        out_specs=vmem,
    )(edge, recv, below, above, tags, inv, fwd)
    got = lax.all_to_all(sent, "span", 0, 0, tiled=True)
    joined = shape(5, 4, total, modes)
    part = call(lambda d, t, c: column_load(d, t, c, elems), joined)(own, got)

    def join(c):
        return lax.ppermute(c[4], "plane", up), lax.ppermute(c[0], "plane", down)

    def row_join(c, lo, hi, prev, theta_ref, v):
        for j in range(5):
            for i in range(4):
                val = c[j, i]
                if j == 0:
                    val = val + lo[i]
                if j == 4:
                    val = val + hi[i]
                if prev is not None:
                    val = val - theta_ref[...] * prev[j, i]
                v[j, i] = val

    row = shape(1, modes)

    def step0(edge_ref, c, lo, hi, th, sh, v, out, sq, dt):
        row_join(c, lo, hi, None, None, v)
        sq[...] = square_sum(v, edge_ref[0] == 1, edge_ref[1] == 1)
        dt[...] = apply_local(v, out, sh[...])

    def step1(edge_ref, c, lo, hi, prev, th, sh, v, out, sq, dt):
        row_join(c, lo, hi, prev, th, v)
        sq[...] = square_sum(v, edge_ref[0] == 1, edge_ref[1] == 1)
        dt[...] = apply_local(v, out, sh[...])

    def finish(edge_ref, c, lo, hi, prev, th, sh, v, sq, dt, out):
        step1(edge_ref, c, lo, hi, prev, th, sh, v, out, sq, dt)

    v0, c1, s0, t0 = call(step0, (joined, joined, row, row), in_specs=[smem] + [vmem] * 5)(
        edge, part, *join(part), theta, shift
    )
    v1, c2, s1, t1 = call(step1, (joined, joined, row, row), in_specs=[smem] + [vmem] * 6)(
        edge, c1, *join(c1), v0, theta, shift
    )
    v2, s2, t2 = call(
        finish,
        (joined, row, row),
        [pltpu.VMEM(joined.shape, f32)],
        in_specs=[smem] + [vmem] * 6,
    )(edge, c2, *join(c2), v1, theta, shift)
    sums = lax.psum(jnp.concatenate([s0, t0, s1, t1, s2, t2], axis=0), "plane")
    n0, h0, n2, h2, n4, h4 = [sums[k : k + 1] for k in range(6)]
    nu = [n0, h0 - theta * n0, n2, h2 - theta * n2, n4, h4 - theta * n4]
    y = jnp.concatenate(solve3(nu, theta), axis=0)
    return call(unpack, shape(modes, rows, cols))(v0, v1, v2, y, expand)


def solution(mesh):
    spec = P("span", "plane", None)
    return jax.shard_map(
        on_device, mesh=mesh, in_specs=(spec, P()), out_specs=spec, check_vma=False
    )
```

```python
import functools
import math

import jax
import jax.numpy as jnp
import numpy as np
from jax import lax
from jax.experimental import pallas as pl
from jax.experimental.pallas import tpu as pltpu
from jax.sharding import PartitionSpec as P

KMODES = 256
PLANES = 768
STEP = 0.03
VISCOUS = 0.05
STIFF = 4.0
PAD = 16

f32 = jnp.float32
bf16 = jnp.bfloat16
NT = (((1,), (1,)), ((), ()))
NN = (((1,), (0,)), ((), ()))
TN = (((0,), (0,)), ((), ()))
VMEM_LIMIT = 56 * 1024 * 1024


def gll_tables():
    x = np.array([-1.0, -math.sqrt(3.0 / 7.0), 0.0, math.sqrt(3.0 / 7.0), 1.0])
    w = np.array([0.1, 49.0 / 90.0, 32.0 / 45.0, 49.0 / 90.0, 0.1])
    q = x * x
    leg = (35.0 * q * q - 30.0 * q + 3.0) / 8.0
    eye = np.eye(5)
    d = np.where(eye > 0, 0.0, leg[:, None] / leg[None, :] / (x[:, None] - x[None, :] + eye))
    d[0, 0], d[4, 4] = -5.0, 5.0
    return d, w, d.T @ (w[:, None] * d)


DIFF, WEIGHT, KMAT = gll_tables()


def halves(table):
    high = table.astype(np.float32).astype(bf16)
    low = (table.astype(np.float32) - high.astype(np.float32)).astype(bf16)
    return high, low


def basis_tables():
    k, p = np.arange(KMODES), np.arange(PLANES)
    angle = 2.0 * math.pi * (p[:, None] * k[None, :] % PLANES) / PLANES
    cos, sin = np.cos(angle), np.sin(angle)
    inverse = np.stack([cos, sin], 2).reshape(PLANES, 2 * KMODES).T / math.sqrt(KMODES)
    factor = np.where(k == 0, 1.0, 2.0) * (math.sqrt(KMODES) / PLANES) * STEP
    ratio = k / KMODES
    inner = np.stack([cos * factor, sin * factor], 2).reshape(PLANES, 2 * KMODES)
    span = np.stack([-ratio * sin * factor, ratio * cos * factor], 2).reshape(PLANES, 2 * KMODES)
    return inverse, inner, span


def split2(x):
    high = x.astype(bf16)
    return high, (x - high.astype(f32)).astype(bf16)


def dot(a, b, dims=NN):
    return lax.dot_general(a, b, dims, preferred_element_type=f32)


def along(mat, a, flip):
    s1, d1, s2, d2, m = a[0] + a[4], a[0] - a[4], a[1] + a[3], a[1] - a[3], a[2]
    out = [None] * 5
    for r in (0, 1):
        e = [0.5 * (mat[r][b] + mat[r][4 - b]) for b in (0, 1)]
        o = [0.5 * (mat[r][b] - mat[r][4 - b]) for b in (0, 1)]
        even = float(e[0]) * s1 + float(e[1]) * s2 + float(mat[r][2]) * m
        odd = float(o[0]) * d1 + float(o[1]) * d2
        out[r] = even + odd
        out[4 - r] = even - odd if flip > 0 else odd - even
    if flip > 0:
        out[2] = float(mat[2][0]) * s1 + float(mat[2][1]) * s2 + float(mat[2][2]) * m
    else:
        out[2] = float(mat[2][0]) * d1 + float(mat[2][1]) * d2
    return out


def two_point10(a, b, qa, qb):
    speed = jnp.maximum(jnp.abs(a), jnp.abs(b))
    return (qa + a * b + qb) * (10.0 / 6.0) - 5.0 * speed * (b - a)


def roll(x, by):
    return pltpu.roll(x, by % x.shape[0], 0)


def pack(x_ref, perm_ref, d_ref, span, elems):
    rows, modes, cols = x_ref.shape
    block = 5 * elems
    parts = split2(x_ref[...].reshape(rows * modes, cols))
    for s in range(span):
        lo = block * s // 128 * 128
        hi = -(-block * (s + 1) // 128) * 128
        perm = perm_ref[s, :, : hi - lo]
        got = sum(dot(perm, part[:, lo:hi], NT) for part in parts)
        for j in range(rows):
            d_ref[s, block * j : block * (j + 1), :] = got[:, modes * j : modes * (j + 1)]
    for s in range(span):
        left, right = (s - 1) % span, (s + 1) % span
        for j in range(rows):
            at = block * rows + 2 * j
            last = block * j + block - 1
            d_ref[s, at : at + 1, :] = d_ref[left, last : last + 1, :]
            d_ref[s, at + 1 : at + 2, :] = d_ref[right, block * j : block * j + 1, :]
        for at in range(block * rows + 2 * rows, block * rows + PAD):
            d_ref[s, at : at + 1, :] = jnp.zeros((1, modes), f32)


def perm_tables(span, elems):
    block = 5 * elems
    width = max(-(-block * (s + 1) // 128) * 128 - block * s // 128 * 128 for s in range(span))
    perm = np.zeros((span, block, width), np.float32)
    for s in range(span):
        lo = block * s // 128 * 128
        for i in range(5):
            for e in range(elems):
                perm[s, i * elems + e, block * s + 5 * e + i - lo] = 1.0
    return perm.astype(bf16)


def to_planes(parts, inv_ref, fld_ref, lo):
    x = jnp.concatenate(
        [jnp.concatenate([p[s] for s in range(p.shape[0])], axis=1) for p in parts], axis=0
    )
    high, low = split2(x)
    for n in range(PLANES // 256):
        at = slice(n * 256, (n + 1) * 256)
        bh, bl = inv_ref[0, :, at], inv_ref[1, :, at]
        fld_ref[lo : lo + x.shape[0], at] = dot(high, bh) + dot(high, bl) + dot(low, bh)


def outer_rows(fld_ref, tag_ref, elems, first, last):
    block = 5 * elems
    sr = 5 * block + PAD

    @pl.when(first)
    def _():
        own = fld_ref[0:block, :]
        fld_ref[sr : sr + block, :] = jnp.where(tag_ref[...] == 1, -own, own)

    @pl.when(last)
    def _():
        fld_ref[sr + block : sr + 2 * block, :] = fld_ref[4 * block : 5 * block, :]


def pointwise(fld_ref, r_ref, h_ref, elems):
    block = 5 * elems
    sr = 5 * block + PAD
    lane = 128
    third = DIFF * (-1.0 / 3.0)

    def body(n, _):
        at = pl.ds(pl.multiple_of(n * lane, lane), lane)
        row = lax.broadcasted_iota(jnp.int32, (elems, lane), 0)

        def load(k):
            return fld_ref[k : k + elems, at]

        u = [[load(block * j + elems * i) for i in range(5)] for j in range(5)]
        q = [[v * v for v in r] for r in u]
        rhs = [[None] * 5 for _ in range(5)]
        for j in range(5):
            du = along(third, u[j], -1)
            dq = along(third, q[j], -1)
            for i in range(5):
                rhs[j][i] = dq[i] + u[j][i] * du[i]
            hl = fld_ref[5 * block + 2 * j : 5 * block + 2 * j + 1, at]
            hr = fld_ref[5 * block + 2 * j + 1 : 5 * block + 2 * j + 2, at]
            left = jnp.where(row == 0, hl, roll(u[j][4], 1))
            right = jnp.where(row == elems - 1, hr, roll(u[j][0], -1))
            rhs[j][0] += two_point10(left, u[j][0], left * left, q[j][0]) - 5.0 * q[j][0]
            rhs[j][4] -= two_point10(u[j][4], right, q[j][4], right * right) - 5.0 * q[j][4]
        for i in range(5):
            ui, qi = [u[j][i] for j in range(5)], [q[j][i] for j in range(5)]
            du = along(third, ui, -1)
            dq = along(third, qi, -1)
            for j in range(5):
                rhs[j][i] += dq[j] + ui[j] * du[j]
            lower = load(sr + elems * i)
            upper = load(sr + block + elems * i)
            rhs[0][i] += two_point10(lower, ui[0], lower * lower, qi[0]) - 5.0 * qi[0]
            rhs[4][i] -= two_point10(ui[4], upper, qi[4], upper * upper) - 5.0 * qi[4]
        for ref, val, scale in ((r_ref, rhs, None), (h_ref, q, 0.5)):
            for j in range(5):
                a = val[j] if scale is None else [scale * v for v in val[j]]
                ref[4 * elems * j : 4 * elems * j + elems, at] = a[0] + jnp.where(
                    row == 0, 0.0, roll(a[4], 1)
                )
                for i in (1, 2, 3):
                    k = elems * (4 * j + i)
                    ref[k : k + elems, at] = a[i]
                ref[20 * elems + j : 20 * elems + j + 1, at] = a[4][elems - 1 : elems, :]
            ref[20 * elems + 5 : 20 * elems + PAD, at] = jnp.zeros((PAD - 5, lane), f32)
        return 0

    lax.fori_loop(0, PLANES // lane, body, 0)


def spectral(r_ref, h_ref, fwd_ref, t_ref):
    span, _, modes = t_ref.shape
    rh, rl = split2(r_ref[...])
    hh, hl = split2(h_ref[...])
    step = max(modes, 256)
    for n in range(span * modes // step):
        at = slice(n * step, (n + 1) * step)
        a, b = fwd_ref[0, :, at], fwd_ref[1, :, at]
        c, d = fwd_ref[2, :, at], fwd_ref[3, :, at]
        t = dot(rh, a) + dot(rl, a) + dot(rh, b) + dot(hh, c) + dot(hl, c) + dot(hh, d)
        for k in range(step // modes):
            t_ref[n * (step // modes) + k] = t[:, modes * k : modes * (k + 1)]


def column_load(d_ref, t_ref, c_ref, elems, js):
    chunks, span, _, modes = t_ref.shape
    blocks = chunks * span
    block = 5 * elems
    row = lax.broadcasted_iota(jnp.int32, (elems, modes), 0)
    for j in js:
        for b in range(blocks):
            s, k = divmod(b, chunks)
            left = (b - 1) % blocks
            sl, kl = divmod(left, chunks)
            for i in range(4):
                at = block * j + elems * i
                tat = elems * (4 * j + i)
                val = d_ref[b, at : at + elems, :] + t_ref[k, s, tat : tat + elems, :]
                if i == 0:
                    at4 = block * j + 4 * elems
                    extra = 20 * elems + j
                    edge = (
                        d_ref[left, at4 + elems - 1 : at4 + elems, :]
                        + t_ref[kl, sl, extra : extra + 1, :]
                    )
                    val += jnp.where(row == 0, edge, roll(d_ref[b, at4 : at4 + elems, :], 1))
                c_ref[j, i, elems * b : elems * (b + 1), :] = val * float(WEIGHT[j] * WEIGHT[i])


def fold(x):
    return jnp.sum(x.reshape(x.shape[0] // 8, 8, x.shape[1]), axis=0)


def image(v_ref, out_ref, shift, js):
    col = [2.0 * WEIGHT[0], WEIGHT[1], WEIGHT[2], WEIGHT[3]]
    for j in js:
        a = [v_ref[j, i] for i in range(4)]
        a.append(roll(a[0], -1))
        kx = along(KMAT * (VISCOUS * WEIGHT[j]), a, 1)
        kx[0] = kx[0] + roll(kx[4], 1)
        for i in range(4):
            out_ref[j, i] = kx[i]
    total = 0.0
    for i in range(4):
        a = [v_ref[j, i] for j in range(5)]
        ky = along(KMAT * (VISCOUS * col[i]), a, 1)
        for j in js:
            val = out_ref[j, i] + ky[j] + (shift * float(WEIGHT[j] * col[i])) * a[j]
            out_ref[j, i] = val
            total = total + fold(val * a[j])
    return total


def join_rows(c_ref, lo, hi, prev, theta, v_ref, first, last):
    total = 0.0
    for j in (0, 4, 1, 2, 3):
        part = 0.0
        for i in range(4):
            val = c_ref[j, i]
            if j == 0:
                val = val + lo[i]
            if j == 4:
                val = val + hi[i]
            if prev is not None:
                val = val - theta * prev[j, i]
            v_ref[j, i] = val
            part = part + fold(val * val)
        if j == 0:
            part = part * jnp.where(first, 1.0, 0.5)
        if j == 4:
            part = part * jnp.where(last, 1.0, 0.5)
        total = total + part
    return total


def solve3(nu, theta):
    a = [[nu[r + c + 1] + theta * nu[r + c] for c in range(3)] for r in range(3)]
    l10, l20 = a[1][0] / a[0][0], a[2][0] / a[0][0]
    d1 = a[1][1] - l10 * a[1][0]
    e = a[2][1] - l20 * a[1][0]
    l21 = e / d1
    d2 = a[2][2] - l20 * a[2][0] - l21 * e
    z0 = nu[0]
    z1 = nu[1] - l10 * z0
    z2 = nu[2] - l20 * z0 - l21 * z1
    y2 = z2 / d2
    y1 = z1 / d1 - l21 * y2
    return z0 / a[0][0] - l10 * y1 - l20 * y2, y1, y2


def unpack(x_ref, exp_ref, out_ref):
    out_ref[0] = sum(dot(part, exp_ref[...], TN) for part in split2(x_ref[0]))


def expand_table(total):
    out = np.zeros((4 * total, 5 * total), np.float32)
    for e in range(total):
        for i in range(5):
            out[(i % 4) * total + (e + i // 4) % total, 5 * e + i] = 1.0
    return out.astype(bf16)


def segment(
    dims, x_ref, perm_ref, tag_ref, shift_ref, theta_ref, inv_hbm, fwd_hbm, out_ref,
    inv, fwd, d_ref, recv, below, above, fld, r_ref, h_ref, tsend, trecv,
    c_ref, v0, v1, v2, lo, hi, part, parts,
    table_sem, s1, r1, s2, r2, s3, r3, s4, r4, s5, r5,
):
    span, planes, chunks, elems = dims
    blocks, bl = span * chunks, 5 * elems
    sr = 5 * bl + PAD
    me, mp = lax.axis_index("span"), lax.axis_index("plane")
    first, last = mp == 0, mp == planes - 1
    inner, beyond = mp > 0, mp < planes - 1
    up, down = {"plane": lax.rem(mp + 1, planes)}, {"plane": lax.rem(mp + planes - 1, planes)}

    def remote(src, dst, send, recv_sem, device):
        return pltpu.make_async_remote_copy(
            src_ref=src, dst_ref=dst, send_sem=send, recv_sem=recv_sem,
            device_id=device, device_id_type=pl.DeviceIdType.MESH,
        )

    def peer(d):
        return lax.rem(me + d, span)

    barrier = pltpu.get_barrier_semaphore()
    for axis, here, count in (("span", me, span), ("plane", mp, planes)):
        for d in range(1, count):
            pl.semaphore_signal(
                barrier, inc=1, device_id={axis: lax.rem(here + d, count)},
                device_id_type=pl.DeviceIdType.MESH,
            )
    tables = [
        pltpu.make_async_copy(inv_hbm, inv, table_sem.at[0]),
        pltpu.make_async_copy(fwd_hbm, fwd, table_sem.at[1]),
    ]
    for copy in tables:
        copy.start()
    pack(x_ref, perm_ref, d_ref, blocks, elems)
    pl.semaphore_wait(barrier, span + planes - 2)

    def state_copy(k, d):
        src = d_ref.at[peer(d) * chunks + k]
        return remote(src, recv.at[k, me], s1.at[k, d - 1], r1.at[k, d - 1], {"span": peer(d)})

    def row_copies(k):
        a = remote(recv.at[k, :, 4 * bl : 5 * bl, :], below.at[k], s2.at[k, 0], r2.at[k, 0], up)
        b = remote(recv.at[k, :, 0:bl, :], above.at[k], s2.at[k, 1], r2.at[k, 1], down)
        return a, b

    def tend_copy(k, d):
        src = tsend.at[k, peer(d)]
        return remote(src, trecv.at[k, me], s3.at[k, d - 1], r3.at[k, d - 1], {"span": peer(d)})

    def join_copies(n):
        a = remote(c_ref.at[4], lo.at[n], s4.at[n, 0], r4.at[n, 0], up)
        b = remote(c_ref.at[0], hi.at[n], s4.at[n, 1], r4.at[n, 1], down)
        return a, b

    def start_pair(pair):
        pl.when(beyond)(pair[0].start)
        pl.when(inner)(pair[1].start)

    def wait_sent(pair):
        pl.when(beyond)(pair[0].wait_send)
        pl.when(inner)(pair[1].wait_send)

    def wait_got(pair):
        pl.when(inner)(pair[0].wait_recv)
        pl.when(beyond)(pair[1].wait_recv)

    for k in range(chunks):
        for d in range(1, span):
            state_copy(k, d).start()
    for k in range(chunks):
        recv[k, me] = d_ref[me * chunks + k]

    @pl.when(first)
    def _():
        below[...] = jnp.zeros_like(below)
        lo[...] = jnp.zeros_like(lo)

    @pl.when(last)
    def _():
        above[...] = jnp.zeros_like(above)
        hi[...] = jnp.zeros_like(hi)

    for k in range(chunks):
        for d in range(1, span):
            state_copy(k, d).wait_recv()
        start_pair(row_copies(k))
        if k == 0:
            for copy in tables:
                copy.wait()
        to_planes([recv.at[k]], inv, fld, 0)
        wait_got(row_copies(k))
        to_planes([below.at[k], above.at[k]], inv, fld, sr)
        outer_rows(fld, tag_ref.at[k], elems, first, last)
        pointwise(fld, r_ref, h_ref, elems)
        spectral(r_ref, h_ref, fwd, tsend.at[k])
        for d in range(1, span):
            tend_copy(k, d).start()
        trecv[k, me] = tsend[k, me]

    for k in range(chunks):
        for d in range(1, span):
            tend_copy(k, d).wait_recv()
    column_load(d_ref, trecv, c_ref, elems, (0, 4))
    start_pair(join_copies(0))
    column_load(d_ref, trecv, c_ref, elems, (1, 2, 3))
    shift, theta = shift_ref[...], theta_ref[...]
    sums = []
    prev = None
    for n, v in enumerate((v0, v1, v2)):
        wait_got(join_copies(n))
        sums.append(join_rows(c_ref, lo.at[n], hi.at[n], prev, theta, v, first, last))
        wait_sent(join_copies(n))
        outer = image(v, c_ref, shift, (0, 4))
        if n < 2:
            start_pair(join_copies(n + 1))
        sums.append(outer + image(v, c_ref, shift, (1, 2, 3)))
        prev = v
    rows = [jnp.sum(t, axis=0, keepdims=True) for t in sums]
    part[...] = jnp.concatenate(rows + [jnp.zeros_like(rows[0])] * 2, axis=0)

    def part_copy(d):
        to = {"plane": lax.rem(mp + d, planes)}
        return remote(part, parts.at[mp], s5.at[d - 1], r5.at[d - 1], to)

    for d in range(1, planes):
        part_copy(d).start()
    parts[mp] = part[...]
    for d in range(1, planes):
        part_copy(d).wait_recv()
    got = jnp.sum(parts[...], axis=0)
    n0, h0, n2, h2, n4, h4 = [got[k : k + 1] for k in range(6)]
    nu = [n0, h0 - theta * n0, n2, h2 - theta * n2, n4, h4 - theta * n4]
    y = solve3(nu, theta)
    total = v0.shape[2]
    for j in range(5):
        for i in range(4):
            out_ref[j, i * total : (i + 1) * total, :] = (
                y[0] * v0[j, i] + y[1] * v1[j, i] + y[2] * v2[j, i]
            )
    for k in range(chunks):
        for d in range(1, span):
            state_copy(k, d).wait_send()
            tend_copy(k, d).wait_send()
        wait_sent(row_copies(k))
    for d in range(1, planes):
        part_copy(d).wait_send()


def shape(*dims):
    return jax.ShapeDtypeStruct(dims, f32)


def on_device(state, wall_tag):
    modes, rows, cols = state.shape
    assert rows == 5
    span, planes = lax.axis_size("span"), lax.axis_size("plane")
    total = cols // 5
    mine = total // span
    chunks = 2 if mine % 16 == 0 else 1
    elems = mine // chunks
    bl = 5 * elems
    sr, tr = 5 * bl + PAD, 20 * elems + PAD
    my_span = lax.axis_index("span")

    inverse, inner, outer = basis_tables()
    inv = jnp.asarray(np.stack(halves(inverse)))
    fwd = jnp.asarray(np.stack(halves(inner) + halves(outer)))
    perm = jnp.asarray(perm_tables(span * chunks, elems))
    expand = jnp.asarray(expand_table(total))
    ids = my_span * modes + jnp.arange(modes, dtype=jnp.int32)
    wave = (ids // 2).astype(f32) / KMODES
    shift = (1.0 + STIFF * wave * wave)[None, :]
    theta = 0.6 + 0.254 * (shift - 1.0)
    tags = lax.dynamic_slice_in_dim(wall_tag, my_span * mine, mine, 0).reshape(chunks, 1, elems)
    tags = jnp.tile(tags, (1, 5, 1)).reshape(chunks, bl, 1)
    vmem = pl.BlockSpec(memory_space=pltpu.VMEM)
    hbm = pl.BlockSpec(memory_space=pl.ANY)
    buf = lambda *d: pltpu.VMEM(d, f32)
    dma = lambda *d: pltpu.SemaphoreType.DMA(d)
    joined = buf(5, 4, total, modes)
    halo = buf(3, 4, total, modes)

    x = pl.pallas_call(
        functools.partial(segment, (span, planes, chunks, elems)),
        out_shape=shape(5, 4 * total, modes),
        in_specs=[vmem] * 5 + [hbm] * 2,
        out_specs=vmem,
        scratch_shapes=[
            pltpu.VMEM(inv.shape, bf16),
            pltpu.VMEM(fwd.shape, bf16),
            buf(span * chunks, sr, modes),
            buf(chunks, span, sr, modes),
            buf(chunks, span, bl, modes),
            buf(chunks, span, bl, modes),
            buf(sr + 2 * bl, PLANES),
            buf(tr, PLANES),
            buf(tr, PLANES),
            buf(chunks, span, tr, modes),
            buf(chunks, span, tr, modes),
            joined, joined, joined, joined, halo, halo,
            buf(8, modes),
            buf(planes, 8, modes),
            dma(2),
            dma(chunks, span - 1), dma(chunks, span - 1),
            dma(chunks, 2), dma(chunks, 2),
            dma(chunks, span - 1), dma(chunks, span - 1),
            dma(3, 2), dma(3, 2),
            dma(planes - 1), dma(planes - 1),
        ],
        compiler_params=pltpu.CompilerParams(
            vmem_limit_bytes=VMEM_LIMIT, collective_id=0, has_side_effects=True
        ),
    )(state.transpose(1, 0, 2), perm, tags, shift, theta, inv, fwd)
    out = pl.pallas_call(
        unpack,
        out_shape=shape(5, modes, cols),
        grid=(5,),
        in_specs=[
            pl.BlockSpec((1, 4 * total, modes), lambda j: (j, 0, 0)),
            pl.BlockSpec(expand.shape, lambda j: (0, 0)),
        ],
        out_specs=pl.BlockSpec((1, modes, cols), lambda j: (j, 0, 0)),
        compiler_params=pltpu.CompilerParams(vmem_limit_bytes=VMEM_LIMIT),
    )(x, expand)
    return out.transpose(1, 0, 2)


def solution(mesh):
    spec = P("span", "plane", None)
    return jax.shard_map(
        on_device, mesh=mesh, in_specs=(spec, P()), out_specs=spec, check_vma=False
    )
```

```python
import functools
import math

import jax
import jax.numpy as jnp
import numpy as np
from jax import lax
from jax.experimental import pallas as pl
from jax.experimental.pallas import tpu as pltpu
from jax.sharding import PartitionSpec as P

KMODES = 256
PLANES = 768
STEP = 0.03
VISCOUS = 0.05
STIFF = 4.0
PAD = 16

f32 = jnp.float32
bf16 = jnp.bfloat16
NT = (((1,), (1,)), ((), ()))
NN = (((1,), (0,)), ((), ()))
TN = (((0,), (0,)), ((), ()))
VMEM_LIMIT = 56 * 1024 * 1024


def gll_tables():
    x = np.array([-1.0, -math.sqrt(3.0 / 7.0), 0.0, math.sqrt(3.0 / 7.0), 1.0])
    w = np.array([0.1, 49.0 / 90.0, 32.0 / 45.0, 49.0 / 90.0, 0.1])
    q = x * x
    leg = (35.0 * q * q - 30.0 * q + 3.0) / 8.0
    eye = np.eye(5)
    d = np.where(eye > 0, 0.0, leg[:, None] / leg[None, :] / (x[:, None] - x[None, :] + eye))
    d[0, 0], d[4, 4] = -5.0, 5.0
    return d, w, d.T @ (w[:, None] * d)


DIFF, WEIGHT, KMAT = gll_tables()


def halves(table):
    high = table.astype(np.float32).astype(bf16)
    low = (table.astype(np.float32) - high.astype(np.float32)).astype(bf16)
    return high, low


def basis_tables():
    k, p = np.arange(KMODES), np.arange(PLANES)
    angle = 2.0 * math.pi * (p[:, None] * k[None, :] % PLANES) / PLANES
    cos, sin = np.cos(angle), np.sin(angle)
    inverse = np.stack([cos, sin], 2).reshape(PLANES, 2 * KMODES).T / math.sqrt(KMODES)
    factor = np.where(k == 0, 1.0, 2.0) * (math.sqrt(KMODES) / PLANES) * STEP
    ratio = k / KMODES
    inner = np.stack([cos * factor, sin * factor], 2).reshape(PLANES, 2 * KMODES)
    span = np.stack([-ratio * sin * factor, ratio * cos * factor], 2).reshape(PLANES, 2 * KMODES)
    return inverse, inner, span


def split2(x):
    high = x.astype(bf16)
    return high, (x - high.astype(f32)).astype(bf16)


def dot(a, b, dims=NN):
    return lax.dot_general(a, b, dims, preferred_element_type=f32)


def along(mat, a, flip):
    s1, d1, s2, d2, m = a[0] + a[4], a[0] - a[4], a[1] + a[3], a[1] - a[3], a[2]
    out = [None] * 5
    for r in (0, 1):
        e = [0.5 * (mat[r][b] + mat[r][4 - b]) for b in (0, 1)]
        o = [0.5 * (mat[r][b] - mat[r][4 - b]) for b in (0, 1)]
        even = float(e[0]) * s1 + float(e[1]) * s2 + float(mat[r][2]) * m
        odd = float(o[0]) * d1 + float(o[1]) * d2
        out[r] = even + odd
        out[4 - r] = even - odd if flip > 0 else odd - even
    if flip > 0:
        out[2] = float(mat[2][0]) * s1 + float(mat[2][1]) * s2 + float(mat[2][2]) * m
    else:
        out[2] = float(mat[2][0]) * d1 + float(mat[2][1]) * d2
    return out


def two_point10(a, b, qa, qb):
    speed = jnp.maximum(jnp.abs(a), jnp.abs(b))
    return (qa + a * b + qb) * (10.0 / 6.0) - 5.0 * speed * (b - a)


def roll(x, by):
    return pltpu.roll(x, by % x.shape[0], 0)


def pack(x_ref, perm_ref, d_ref, span, chunks, elems):
    rows, modes, cols = x_ref.shape
    block = 5 * elems
    wide = block * chunks
    blocks = span * chunks
    parts = split2(x_ref[...].reshape(rows * modes, cols))
    for s in range(span):
        lo = wide * s // 128 * 128
        hi = -(-wide * (s + 1) // 128) * 128
        perm = perm_ref[s, :, : hi - lo]
        got = sum(dot(perm, part[:, lo:hi], NT) for part in parts)
        for k in range(chunks):
            for j in range(rows):
                d_ref[s * chunks + k, block * j : block * (j + 1), :] = got[
                    block * k : block * (k + 1), modes * j : modes * (j + 1)
                ]
    for b in range(blocks):
        left, right = (b - 1) % blocks, (b + 1) % blocks
        for j in range(rows):
            at = block * rows + 2 * j
            last = block * j + block - 1
            d_ref[b, at : at + 1, :] = d_ref[left, last : last + 1, :]
            d_ref[b, at + 1 : at + 2, :] = d_ref[right, block * j : block * j + 1, :]
        at = block * rows + 2 * rows
        d_ref[b, at : block * rows + PAD, :] = jnp.zeros((PAD - 2 * rows, modes), f32)


def perm_tables(span, chunks, elems):
    wide = 5 * elems * chunks
    width = max(-(-wide * (s + 1) // 128) * 128 - wide * s // 128 * 128 for s in range(span))
    perm = np.zeros((span, wide, width), np.float32)
    for s in range(span):
        lo = wide * s // 128 * 128
        for k in range(chunks):
            for i in range(5):
                for e in range(elems):
                    row = (k * 5 + i) * elems + e
                    perm[s, row, wide * s + 5 * (k * elems + e) + i - lo] = 1.0
    return perm.astype(bf16)


def to_planes(parts, inv_ref, fld_ref, lo):
    x = jnp.concatenate(
        [jnp.concatenate([p[s] for s in range(p.shape[0])], axis=1) for p in parts], axis=0
    )
    high, low = split2(x)
    for n in range(PLANES // 256):
        at = slice(n * 256, (n + 1) * 256)
        bh, bl = inv_ref[0, :, at], inv_ref[1, :, at]
        fld_ref[lo : lo + x.shape[0], at] = dot(high, bh) + dot(high, bl) + dot(low, bh)


def outer_rows(fld_ref, tag, elems, first, last):
    block = 5 * elems
    sr = 5 * block + PAD

    @pl.when(first)
    def _():
        own = fld_ref[0:block, :]
        fld_ref[sr : sr + block, :] = jnp.where(tag == 1, -own, own)

    @pl.when(last)
    def _():
        fld_ref[sr + block : sr + 2 * block, :] = fld_ref[4 * block : 5 * block, :]


def pointwise(fld_ref, r_ref, h_ref, elems):
    block = 5 * elems
    sr = 5 * block + PAD
    lane = 128
    third = DIFF * (-1.0 / 3.0)

    def body(n, _):
        at = pl.ds(pl.multiple_of(n * lane, lane), lane)
        row = lax.broadcasted_iota(jnp.int32, (elems, lane), 0)

        def load(k):
            return fld_ref[k : k + elems, at]

        u = [[load(block * j + elems * i) for i in range(5)] for j in range(5)]
        q = [[v * v for v in r] for r in u]
        rhs = [[None] * 5 for _ in range(5)]
        for j in range(5):
            du = along(third, u[j], -1)
            dq = along(third, q[j], -1)
            for i in range(5):
                rhs[j][i] = dq[i] + u[j][i] * du[i]
            hl = fld_ref[5 * block + 2 * j : 5 * block + 2 * j + 1, at]
            hr = fld_ref[5 * block + 2 * j + 1 : 5 * block + 2 * j + 2, at]
            left = jnp.where(row == 0, hl, roll(u[j][4], 1))
            right = jnp.where(row == elems - 1, hr, roll(u[j][0], -1))
            rhs[j][0] += two_point10(left, u[j][0], left * left, q[j][0]) - 5.0 * q[j][0]
            rhs[j][4] -= two_point10(u[j][4], right, q[j][4], right * right) - 5.0 * q[j][4]
        for i in range(5):
            ui, qi = [u[j][i] for j in range(5)], [q[j][i] for j in range(5)]
            du = along(third, ui, -1)
            dq = along(third, qi, -1)
            for j in range(5):
                rhs[j][i] += dq[j] + ui[j] * du[j]
            lower = load(sr + elems * i)
            upper = load(sr + block + elems * i)
            rhs[0][i] += two_point10(lower, ui[0], lower * lower, qi[0]) - 5.0 * qi[0]
            rhs[4][i] -= two_point10(ui[4], upper, qi[4], upper * upper) - 5.0 * qi[4]
        for ref, val, scale in ((r_ref, rhs, None), (h_ref, q, 0.5)):
            for j in range(5):
                a = val[j] if scale is None else [scale * v for v in val[j]]
                ref[4 * elems * j : 4 * elems * j + elems, at] = a[0] + jnp.where(
                    row == 0, 0.0, roll(a[4], 1)
                )
                for i in (1, 2, 3):
                    k = elems * (4 * j + i)
                    ref[k : k + elems, at] = a[i]
                ref[20 * elems + j : 20 * elems + j + 1, at] = a[4][elems - 1 : elems, :]
            ref[20 * elems + 5 : 20 * elems + PAD, at] = jnp.zeros((PAD - 5, lane), f32)
        return 0

    lax.fori_loop(0, PLANES // lane, body, 0)


def spectral(r_ref, h_ref, fwd_ref, t_ref, send):
    span, _, modes = t_ref.shape
    rh, rl = split2(r_ref[...])
    hh, hl = split2(h_ref[...])
    step = max(modes, 256)
    for n in range(span * modes // step):
        at = slice(n * step, (n + 1) * step)
        a, b = fwd_ref[0, :, at], fwd_ref[1, :, at]
        c, d = fwd_ref[2, :, at], fwd_ref[3, :, at]
        t = dot(rh, a) + dot(rl, a) + dot(rh, b) + dot(hh, c) + dot(hl, c) + dot(hh, d)
        for k in range(step // modes):
            s = n * (step // modes) + k
            t_ref[s] = t[:, modes * k : modes * (k + 1)]
            send(s)


def column_load(d_ref, t_ref, c_ref, elems, js):
    chunks, span, _, modes = t_ref.shape
    blocks = chunks * span
    block = 5 * elems
    row = lax.broadcasted_iota(jnp.int32, (elems, modes), 0)
    for j in js:
        for b in range(blocks):
            s, k = divmod(b, chunks)
            left = (b - 1) % blocks
            sl, kl = divmod(left, chunks)
            for i in range(4):
                at = block * j + elems * i
                tat = elems * (4 * j + i)
                val = d_ref[b, at : at + elems, :] + t_ref[k, s, tat : tat + elems, :]
                if i == 0:
                    at4 = block * j + 4 * elems
                    extra = 20 * elems + j
                    edge = (
                        d_ref[left, at4 + elems - 1 : at4 + elems, :]
                        + t_ref[kl, sl, extra : extra + 1, :]
                    )
                    val += jnp.where(row == 0, edge, roll(d_ref[b, at4 : at4 + elems, :], 1))
                c_ref[j, i, elems * b : elems * (b + 1), :] = val * float(WEIGHT[j] * WEIGHT[i])


def fold(x):
    return jnp.sum(x.reshape(x.shape[0] // 8, 8, x.shape[1]), axis=0)


COLW = [2.0 * WEIGHT[0], WEIGHT[1], WEIGHT[2], WEIGHT[3]]


def stretch(v_ref, out_ref, js):
    for j in js:
        a = [v_ref[j, i] for i in range(4)]
        a.append(roll(a[0], -1))
        kx = along(KMAT * (VISCOUS * WEIGHT[j]), a, 1)
        kx[0] = kx[0] + roll(kx[4], 1)
        for i in range(4):
            out_ref[j, i] = kx[i]


def image(v_ref, out_ref, shift, js):
    total = 0.0
    for i in range(4):
        a = [v_ref[j, i] for j in range(5)]
        ky = along(KMAT * (VISCOUS * COLW[i]), a, 1)
        for j in js:
            val = out_ref[j, i] + ky[j] + (shift * float(WEIGHT[j] * COLW[i])) * a[j]
            out_ref[j, i] = val
            total = total + fold(val * a[j])
    return total


def join_rows(c_ref, lo, hi, prev, theta, v_ref, first, last, js):
    total = 0.0
    for j in js:
        part = 0.0
        for i in range(4):
            val = c_ref[j, i]
            if j == 0:
                val = val + lo[i]
            if j == 4:
                val = val + hi[i]
            if prev is not None:
                val = val - theta * prev[j, i]
            v_ref[j, i] = val
            part = part + fold(val * val)
        if j == 0:
            part = part * jnp.where(first, 1.0, 0.5)
        if j == 4:
            part = part * jnp.where(last, 1.0, 0.5)
        total = total + part
    return total


def solve3(nu, theta):
    a = [[nu[r + c + 1] + theta * nu[r + c] for c in range(3)] for r in range(3)]
    l10, l20 = a[1][0] / a[0][0], a[2][0] / a[0][0]
    d1 = a[1][1] - l10 * a[1][0]
    e = a[2][1] - l20 * a[1][0]
    l21 = e / d1
    d2 = a[2][2] - l20 * a[2][0] - l21 * e
    z0 = nu[0]
    z1 = nu[1] - l10 * z0
    z2 = nu[2] - l20 * z0 - l21 * z1
    y2 = z2 / d2
    y1 = z1 / d1 - l21 * y2
    return z0 / a[0][0] - l10 * y1 - l20 * y2, y1, y2


def unpack(v_ref, exp_ref, out_ref):
    rows, four, total, modes = v_ref.shape
    x = jnp.concatenate([v_ref[j].reshape(four * total, modes) for j in range(rows)], axis=1)
    full = sum(dot(part, exp_ref[...], TN) for part in split2(x))
    out_ref[...] = full.reshape(out_ref.shape)


def expand_table(total):
    out = np.zeros((4 * total, 5 * total), np.float32)
    for e in range(total):
        for i in range(5):
            out[(i % 4) * total + (e + i // 4) % total, 5 * e + i] = 1.0
    return out.astype(bf16)


def segment(
    dims, x_ref, perm_ref, tag_ref, inv_hbm, fwd_hbm, exp_hbm, out_ref,
    inv, fwd, expand, w0, w1, w2, d_ref, recv, below, above, fld, r_ref, h_ref, tsend, trecv,
    c_ref, v0, v1, v2, lo, hi, part, parts,
    table_sem, s1, r1, s2, r2, s3, r3, s4, r4, s5, r5,
):
    span, planes, chunks, elems = dims
    modes, bl = x_ref.shape[1], 5 * elems
    sr = 5 * bl + PAD
    me, mp = lax.axis_index("span"), lax.axis_index("plane")
    first, last = mp == 0, mp == planes - 1
    inner, beyond = mp > 0, mp < planes - 1
    up, down = {"plane": lax.rem(mp + 1, planes)}, {"plane": lax.rem(mp + planes - 1, planes)}

    def remote(src, dst, send, recv_sem, device):
        return pltpu.make_async_remote_copy(
            src_ref=src, dst_ref=dst, send_sem=send, recv_sem=recv_sem,
            device_id=device, device_id_type=pl.DeviceIdType.MESH,
        )

    def peer(d):
        return lax.rem(me + d, span)

    barrier = pltpu.get_barrier_semaphore()
    for axis, here, count in (("span", me, span), ("plane", mp, planes)):
        for d in range(1, count):
            pl.semaphore_signal(
                barrier, inc=1, device_id={axis: lax.rem(here + d, count)},
                device_id_type=pl.DeviceIdType.MESH,
            )
    tables = [
        pltpu.make_async_copy(inv_hbm, inv, table_sem.at[0]),
        pltpu.make_async_copy(fwd_hbm, fwd, table_sem.at[1]),
        pltpu.make_async_copy(exp_hbm, expand, table_sem.at[2]),
    ]
    for copy in tables:
        copy.start()
    pack(x_ref, perm_ref, d_ref, span, chunks, elems)
    pl.semaphore_wait(barrier, span + planes - 2)

    def state_copy(k, d):
        src = d_ref.at[peer(d) * chunks + k]
        return remote(src, recv.at[k, me], s1.at[k, d - 1], r1.at[k, d - 1], {"span": peer(d)})

    def row_copies(k):
        a = remote(recv.at[k, :, 4 * bl : 5 * bl, :], below.at[k], s2.at[k, 0], r2.at[k, 0], up)
        b = remote(recv.at[k, :, 0:bl, :], above.at[k], s2.at[k, 1], r2.at[k, 1], down)
        return a, b

    def tend_copy(k, d):
        src = tsend.at[k, peer(d)]
        return remote(src, trecv.at[k, me], s3.at[k, d - 1], r3.at[k, d - 1], {"span": peer(d)})

    def tend_start(k, s):
        off = lax.rem(s - me + span, span)

        @pl.when(off > 0)
        def _():
            remote(
                tsend.at[k, s], trecv.at[k, me], s3.at[k, off - 1], r3.at[k, off - 1], {"span": s}
            ).start()

    def tags(k):
        total = tag_ref.shape[1]
        element = lax.broadcasted_iota(jnp.int32, (elems, total), 0) + (me * chunks + k) * elems
        lane = lax.broadcasted_iota(jnp.int32, (elems, total), 1)
        column = jnp.sum(jnp.where(element == lane, tag_ref[...], 0), axis=1, keepdims=True)
        return jnp.concatenate([column] * 5, axis=0)

    def join_copies(n):
        a = remote(c_ref.at[4], lo.at[n], s4.at[n, 0], r4.at[n, 0], up)
        b = remote(c_ref.at[0], hi.at[n], s4.at[n, 1], r4.at[n, 1], down)
        return a, b

    def start_pair(pair):
        pl.when(beyond)(pair[0].start)
        pl.when(inner)(pair[1].start)

    def wait_sent(pair):
        pl.when(beyond)(pair[0].wait_send)
        pl.when(inner)(pair[1].wait_send)

    def wait_got(pair):
        pl.when(inner)(pair[0].wait_recv)
        pl.when(beyond)(pair[1].wait_recv)

    for k in range(chunks):
        for d in range(1, span):
            state_copy(k, d).start()
    for k in range(chunks):
        recv[k, me] = d_ref[me * chunks + k]

    @pl.when(first)
    def _():
        below[...] = jnp.zeros_like(below)
        lo[...] = jnp.zeros_like(lo)

    @pl.when(last)
    def _():
        above[...] = jnp.zeros_like(above)
        hi[...] = jnp.zeros_like(hi)

    for k in range(chunks):
        for d in range(1, span):
            state_copy(k, d).wait_recv()
        start_pair(row_copies(k))
        if k == 0:
            for copy in tables:
                copy.wait()
        to_planes([recv.at[k]], inv, fld, 0)
        wait_got(row_copies(k))
        to_planes([below.at[k], above.at[k]], inv, fld, sr)
        outer_rows(fld, tags(k), elems, first, last)
        pointwise(fld, r_ref, h_ref, elems)
        spectral(r_ref, h_ref, fwd, tsend.at[k], functools.partial(tend_start, k))
        trecv[k, me] = tsend[k, me]

    for k in range(chunks):
        for d in range(1, span):
            tend_copy(k, d).wait_recv()
    column_load(d_ref, trecv, c_ref, elems, (0, 4))
    start_pair(join_copies(0))
    column_load(d_ref, trecv, c_ref, elems, (1, 2, 3))
    ids = me * modes + lax.broadcasted_iota(jnp.int32, (1, modes), 1)
    wave = lax.shift_right_logical(ids, 1).astype(f32) / KMODES
    shift = 1.0 + STIFF * wave * wave
    theta = 0.6 + 0.254 * (shift - 1.0)
    sums = []
    prev = None
    for n, (v, w) in enumerate(((v0, w0), (v1, w1), (v2, w2))):
        join = functools.partial(
            join_rows, c_ref, lo.at[n], hi.at[n], prev, theta, v, first, last
        )
        square = join((1, 2, 3))
        stretch(v, c_ref, (1, 2, 3))
        wait_got(join_copies(n))
        sums.append(square + join((0, 4)))
        wait_sent(join_copies(n))
        stretch(v, c_ref, (0, 4))
        outer = image(v, c_ref, shift, (0, 4))
        if n < 2:
            start_pair(join_copies(n + 1))
        sums.append(outer + image(v, c_ref, shift, (1, 2, 3)))
        if n < 2:
            unpack(v, expand, w)
        prev = v
    rows = [jnp.sum(t, axis=0, keepdims=True) for t in sums]
    part[...] = jnp.concatenate(rows + [jnp.zeros_like(rows[0])] * 2, axis=0)

    def part_copy(d):
        to = {"plane": lax.rem(mp + d, planes)}
        return remote(part, parts.at[mp], s5.at[d - 1], r5.at[d - 1], to)

    for d in range(1, planes):
        part_copy(d).start()
    parts[mp] = part[...]
    unpack(v2, expand, w2)
    for d in range(1, planes):
        part_copy(d).wait_recv()
    got = jnp.sum(parts[...], axis=0)
    n0, h0, n2, h2, n4, h4 = [got[k : k + 1] for k in range(6)]
    nu = [n0, h0 - theta * n0, n2, h2 - theta * n2, n4, h4 - theta * n4]
    y = solve3(nu, theta)
    y = jnp.concatenate(list(y) + [jnp.zeros_like(y[0])] * 5, axis=0).T
    y0, y1, y2 = y[:, 0:1], y[:, 1:2], y[:, 2:3]
    for j in range(5):
        out_ref[j] = y0 * w0[j] + y1 * w1[j] + y2 * w2[j]
    for k in range(chunks):
        for d in range(1, span):
            state_copy(k, d).wait_send()
            tend_copy(k, d).wait_send()
        wait_sent(row_copies(k))
    for d in range(1, planes):
        part_copy(d).wait_send()


def shape(*dims):
    return jax.ShapeDtypeStruct(dims, f32)


def on_device(state, wall_tag):
    modes, rows, cols = state.shape
    assert rows == 5
    span, planes = lax.axis_size("span"), lax.axis_size("plane")
    total = cols // 5
    mine = total // span
    chunks = mine // 8
    elems = mine // chunks
    bl = 5 * elems
    sr, tr = 5 * bl + PAD, 20 * elems + PAD
    inverse, inner, outer = basis_tables()
    inv = jnp.asarray(np.stack(halves(inverse)))
    fwd = jnp.asarray(np.stack(halves(inner) + halves(outer)))
    perm = jnp.asarray(perm_tables(span, chunks, elems))
    expand = jnp.asarray(expand_table(total))
    vmem = pl.BlockSpec(memory_space=pltpu.VMEM)
    hbm = pl.BlockSpec(memory_space=pl.ANY)
    buf = lambda *d: pltpu.VMEM(d, f32)
    dma = lambda *d: pltpu.SemaphoreType.DMA(d)
    joined = buf(5, 4, total, modes)
    halo = buf(3, 4, total, modes)

    out = pl.pallas_call(
        functools.partial(segment, (span, planes, chunks, elems)),
        out_shape=shape(5, modes, cols),
        in_specs=[vmem] * 3 + [hbm] * 3,
        out_specs=vmem,
        scratch_shapes=[
            pltpu.VMEM(inv.shape, bf16),
            pltpu.VMEM(fwd.shape, bf16),
            pltpu.VMEM(expand.shape, bf16),
            buf(5, modes, cols), buf(5, modes, cols), buf(5, modes, cols),
            buf(span * chunks, sr, modes),
            buf(chunks, span, sr, modes),
            buf(chunks, span, bl, modes),
            buf(chunks, span, bl, modes),
            buf(sr + 2 * bl, PLANES),
            buf(tr, PLANES),
            buf(tr, PLANES),
            buf(chunks, span, tr, modes),
            buf(chunks, span, tr, modes),
            joined, joined, joined, joined, halo, halo,
            buf(8, modes),
            buf(planes, 8, modes),
            dma(3),
            dma(chunks, span - 1), dma(chunks, span - 1),
            dma(chunks, 2), dma(chunks, 2),
            dma(chunks, span - 1), dma(chunks, span - 1),
            dma(3, 2), dma(3, 2),
            dma(planes - 1), dma(planes - 1),
        ],
        compiler_params=pltpu.CompilerParams(
            vmem_limit_bytes=VMEM_LIMIT, collective_id=0, has_side_effects=True
        ),
    )(state.transpose(1, 0, 2), perm, wall_tag.reshape(1, total), inv, fwd, expand)
    return out.transpose(1, 0, 2)


def solution(mesh):
    spec = P("span", "plane", None)
    return jax.shard_map(
        on_device, mesh=mesh, in_specs=(spec, P()), out_specs=spec, check_vma=False
    )
```

```python
import functools
import math

import jax
import jax.numpy as jnp
import numpy as np
from jax import lax
from jax.experimental import pallas as pl
from jax.experimental.pallas import tpu as pltpu
from jax.sharding import PartitionSpec as P

KMODES = 256
PLANES = 768
STEP = 0.03
VISCOUS = 0.05
STIFF = 4.0

f32 = jnp.float32
bf16 = jnp.bfloat16
NT = (((1,), (1,)), ((), ()))
NN = (((1,), (0,)), ((), ()))
TN = (((0,), (0,)), ((), ()))
VMEM_LIMIT = 56 * 1024 * 1024


def gll_tables():
    x = np.array([-1.0, -math.sqrt(3.0 / 7.0), 0.0, math.sqrt(3.0 / 7.0), 1.0])
    w = np.array([0.1, 49.0 / 90.0, 32.0 / 45.0, 49.0 / 90.0, 0.1])
    q = x * x
    leg = (35.0 * q * q - 30.0 * q + 3.0) / 8.0
    eye = np.eye(5)
    d = np.where(eye > 0, 0.0, leg[:, None] / leg[None, :] / (x[:, None] - x[None, :] + eye))
    d[0, 0], d[4, 4] = -5.0, 5.0
    return d, w, d.T @ (w[:, None] * d)


DIFF, WEIGHT, KMAT = gll_tables()


def halves(table):
    high = table.astype(np.float32).astype(bf16)
    low = (table.astype(np.float32) - high.astype(np.float32)).astype(bf16)
    return high, low


def basis_tables():
    k, p = np.arange(KMODES), np.arange(PLANES)
    angle = 2.0 * math.pi * (p[:, None] * k[None, :] % PLANES) / PLANES
    cos, sin = np.cos(angle), np.sin(angle)
    inverse = np.stack([cos, sin], 2).reshape(PLANES, 2 * KMODES).T / math.sqrt(KMODES)
    factor = np.where(k == 0, 1.0, 2.0) * (math.sqrt(KMODES) / PLANES) * STEP
    ratio = k / KMODES
    inner = np.stack([cos * factor, sin * factor], 2).reshape(PLANES, 2 * KMODES)
    span = np.stack([-ratio * sin * factor, ratio * cos * factor], 2).reshape(PLANES, 2 * KMODES)
    return inverse, inner, span


def split2(x):
    high = x.astype(bf16)
    return high, (x - high.astype(f32)).astype(bf16)


def dot(a, b, dims=NN):
    return lax.dot_general(a, b, dims, preferred_element_type=f32)


def along(mat, a, flip):
    s1, d1, s2, d2, m = a[0] + a[4], a[0] - a[4], a[1] + a[3], a[1] - a[3], a[2]
    out = [None] * 5
    for r in (0, 1):
        e = [0.5 * (mat[r][b] + mat[r][4 - b]) for b in (0, 1)]
        o = [0.5 * (mat[r][b] - mat[r][4 - b]) for b in (0, 1)]
        even = float(e[0]) * s1 + float(e[1]) * s2 + float(mat[r][2]) * m
        odd = float(o[0]) * d1 + float(o[1]) * d2
        out[r] = even + odd
        out[4 - r] = even - odd if flip > 0 else odd - even
    if flip > 0:
        out[2] = float(mat[2][0]) * s1 + float(mat[2][1]) * s2 + float(mat[2][2]) * m
    else:
        out[2] = float(mat[2][0]) * d1 + float(mat[2][1]) * d2
    return out


def two_point10(a, b, qa, qb):
    speed = jnp.maximum(jnp.abs(a), jnp.abs(b))
    return (qa + a * b + qb) * (10.0 / 6.0) - 5.0 * speed * (b - a)


def roll(x, by):
    return pltpu.roll(x, by % x.shape[0], 0)


def pack(x_ref, perm_ref, d_ref, halo_ref, span, chunks, elems, ready):
    rows, modes, cols = x_ref.shape
    block = 5 * elems
    wide = block * chunks
    blocks = span * chunks
    parts = split2(x_ref[...].reshape(rows * modes, cols))
    for s in range(span):
        lo = wide * s // 128 * 128
        hi = -(-wide * (s + 1) // 128) * 128
        perm = perm_ref[s, :, : hi - lo]
        got = sum(dot(perm, part[:, lo:hi], NT) for part in parts)
        for k in range(chunks):
            for j in range(rows):
                d_ref[s * chunks + k, block * j : block * (j + 1), :] = got[
                    block * k : block * (k + 1), modes * j : modes * (j + 1)
                ]
        ready(s)
    for s in range(span):
        left = (s * chunks - 1) % blocks
        for j in range(rows):
            last = block * j + block - 1
            halo_ref[s, j : j + 1, :] = d_ref[left, last : last + 1, :]
            for k in range(chunks):
                right = (s * chunks + k + 1) % blocks
                at = rows * (k + 1) + j
                halo_ref[s, at : at + 1, :] = d_ref[right, block * j : block * j + 1, :]
        used = rows * (chunks + 1)
        halo_ref[s, used:, :] = jnp.zeros((halo_ref.shape[1] - used, modes), f32)


def perm_tables(span, chunks, elems):
    wide = 5 * elems * chunks
    width = max(-(-wide * (s + 1) // 128) * 128 - wide * s // 128 * 128 for s in range(span))
    perm = np.zeros((span, wide, width), np.float32)
    for s in range(span):
        lo = wide * s // 128 * 128
        for k in range(chunks):
            for i in range(5):
                for e in range(elems):
                    row = (k * 5 + i) * elems + e
                    perm[s, row, wide * s + 5 * (k * elems + e) + i - lo] = 1.0
    return perm.astype(bf16)


def to_planes(parts, inv_ref, fld_ref, lo):
    x = jnp.concatenate(
        [jnp.concatenate([p[s] for s in range(p.shape[0])], axis=1) for p in parts], axis=0
    )
    high, low = split2(x)
    for n in range(PLANES // 256):
        at = slice(n * 256, (n + 1) * 256)
        bh, bl = inv_ref[0, :, at], inv_ref[1, :, at]
        fld_ref[lo : lo + x.shape[0], at] = dot(high, bh) + dot(high, bl) + dot(low, bh)


def outer_rows(fld_ref, tag, elems, first, last):
    block = 5 * elems
    sr = 5 * block

    @pl.when(first)
    def _():
        own = fld_ref[0:block, :]
        fld_ref[sr : sr + block, :] = jnp.where(tag == 1, -own, own)

    @pl.when(last)
    def _():
        fld_ref[sr + block : sr + 2 * block, :] = fld_ref[4 * block : 5 * block, :]


def pointwise(fld_ref, halo_ref, edge_ref, carry_ref, r_ref, h_ref, elems, k, chunks):
    block = 5 * elems
    sr = 5 * block
    lane = 128
    place = {0: 0, 4: 4 * elems}
    for j in (1, 2, 3):
        place[j] = 4 * elems * (j + 1) + 8
    third = DIFF * (-1.0 / 3.0)

    def body(n, _):
        at = pl.ds(pl.multiple_of(n * lane, lane), lane)
        row = lax.broadcasted_iota(jnp.int32, (elems, lane), 0)

        def load(base):
            return fld_ref[base : base + elems, at]

        u = [[load(block * j + elems * i) for i in range(5)] for j in range(5)]
        q = [[v * v for v in r] for r in u]
        rhs = [[None] * 5 for _ in range(5)]
        for j in range(5):
            du = along(third, u[j], -1)
            dq = along(third, q[j], -1)
            for i in range(5):
                rhs[j][i] = dq[i] + u[j][i] * du[i]
            hl = halo_ref[j : j + 1, at] if k == 0 else edge_ref[j : j + 1, at]
            hr = halo_ref[5 * (k + 1) + j : 5 * (k + 1) + j + 1, at]
            edge_ref[j : j + 1, at] = u[j][4][elems - 1 : elems, :]
            left = jnp.where(row == 0, hl, roll(u[j][4], 1))
            right = jnp.where(row == elems - 1, hr, roll(u[j][0], -1))
            rhs[j][0] += two_point10(left, u[j][0], left * left, q[j][0]) - 5.0 * q[j][0]
            rhs[j][4] -= two_point10(u[j][4], right, q[j][4], right * right) - 5.0 * q[j][4]
        for i in range(5):
            ui, qi = [u[j][i] for j in range(5)], [q[j][i] for j in range(5)]
            du = along(third, ui, -1)
            dq = along(third, qi, -1)
            for j in range(5):
                rhs[j][i] += dq[j] + ui[j] * du[j]
            lower = load(sr + elems * i)
            upper = load(sr + block + elems * i)
            rhs[0][i] += two_point10(lower, ui[0], lower * lower, qi[0]) - 5.0 * qi[0]
            rhs[4][i] -= two_point10(ui[4], upper, qi[4], upper * upper) - 5.0 * qi[4]
        for ref, val, scale, base in ((r_ref, rhs, None, 0), (h_ref, q, 0.5, 5)):
            for n, j in enumerate((0, 4, 1, 2, 3)):
                a = val[j] if scale is None else [scale * v for v in val[j]]
                kept = 0.0 if k == 0 else carry_ref[base + j : base + j + 1, at]
                ref[place[j] : place[j] + elems, at] = a[0] + jnp.where(
                    row == 0, kept, roll(a[4], 1)
                )
                for i in (1, 2, 3):
                    to = place[j] + elems * i
                    ref[to : to + elems, at] = a[i]
                tail = a[4][elems - 1 : elems, :]
                if k == chunks - 1:
                    ref[8 * elems + n : 8 * elems + n + 1, at] = tail
                else:
                    carry_ref[base + j : base + j + 1, at] = tail
            if k == chunks - 1:
                ref[8 * elems + 5 : 8 * elems + 8, at] = jnp.zeros((3, lane), f32)
            else:
                ref[8 * elems : 8 * elems + 8, at] = jnp.zeros((8, lane), f32)
        return 0

    lax.fori_loop(0, PLANES // lane, body, 0)


def spectral(r_ref, h_ref, fwd_ref, t_ref, send):
    span, _, modes = t_ref.shape
    rh, rl = split2(r_ref[...])
    hh, hl = split2(h_ref[...])
    step = max(modes, 256)
    for n in range(span * modes // step):
        at = slice(n * step, (n + 1) * step)
        a, b = fwd_ref[0, :, at], fwd_ref[1, :, at]
        c, d = fwd_ref[2, :, at], fwd_ref[3, :, at]
        t = dot(rh, a) + dot(rl, a) + dot(rh, b) + dot(hh, c) + dot(hl, c) + dot(hh, d)
        for k in range(step // modes):
            s = n * (step // modes) + k
            t_ref[s] = t[:, modes * k : modes * (k + 1)]
            send(s)


def column_load(d_ref, c_ref, elems, js):
    blocks, _, modes = d_ref.shape
    block = 5 * elems
    row = lax.broadcasted_iota(jnp.int32, (elems, modes), 0)
    for j in js:
        for b in range(blocks):
            left = (b - 1) % blocks
            for i in range(4):
                at = block * j + elems * i
                val = d_ref[b, at : at + elems, :]
                if i == 0:
                    at4 = block * j + 4 * elems
                    edge = d_ref[left, at4 + elems - 1 : at4 + elems, :]
                    val += jnp.where(row == 0, edge, roll(d_ref[b, at4 : at4 + elems, :], 1))
                c_ref[j, i, elems * b : elems * (b + 1), :] = val * float(WEIGHT[j] * WEIGHT[i])


def add_tendency(v_ref, t_ref, elems, k, chunks):
    span = t_ref.shape[1]
    for j in range(5):
        base = {0: 0, 4: 4 * elems}.get(j, 4 * elems * (j + 1) + 8)
        for s in range(span):
            at = slice(elems * (s * chunks + k), elems * (s * chunks + k + 1))
            for i in range(4):
                part = t_ref[k, s, base + elems * i : base + elems * (i + 1), :]
                v_ref[j, i, at, :] += part * float(WEIGHT[j] * WEIGHT[i])


def add_ends(v_ref, t_ref, elems, chunks):
    span = t_ref.shape[1]
    for n, j in enumerate((0, 4, 1, 2, 3)):
        for s in range(span):
            end = t_ref[chunks - 1, (s - 1) % span, 8 * elems + n : 8 * elems + n + 1, :]
            at = elems * s * chunks
            v_ref[j, 0, at : at + 1, :] += end * float(WEIGHT[j] * WEIGHT[0])


def fold(x):
    return jnp.sum(x.reshape(x.shape[0] // 8, 8, x.shape[1]), axis=0)


COLW = [2.0 * WEIGHT[0], WEIGHT[1], WEIGHT[2], WEIGHT[3]]


def stretch(v_ref, out_ref, js):
    for j in js:
        a = [v_ref[j, i] for i in range(4)]
        a.append(roll(a[0], -1))
        kx = along(KMAT * (VISCOUS * WEIGHT[j]), a, 1)
        kx[0] = kx[0] + roll(kx[4], 1)
        for i in range(4):
            out_ref[j, i] = kx[i]


def image(v_ref, out_ref, shift, js):
    total = 0.0
    for i in range(4):
        a = [v_ref[j, i] for j in range(5)]
        ky = along(KMAT * (VISCOUS * COLW[i]), a, 1)
        for j in js:
            val = out_ref[j, i] + ky[j] + (shift * float(WEIGHT[j] * COLW[i])) * a[j]
            out_ref[j, i] = val
            total = total + fold(val * a[j])
    return total


def join_rows(c_ref, lo, hi, prev, theta, v_ref, js):
    for j in js:
        for i in range(4):
            val = c_ref[j, i]
            if j == 0:
                val = val + lo[i]
            if j == 4:
                val = val + hi[i]
            if prev is not None:
                val = val - theta * prev[j, i]
            v_ref[j, i] = val


def squares(v_ref, first, last, js):
    total = 0.0
    for j in js:
        part = sum(fold(v_ref[j, i] * v_ref[j, i]) for i in range(4))
        if j == 0:
            part = part * jnp.where(first, 1.0, 0.5)
        if j == 4:
            part = part * jnp.where(last, 1.0, 0.5)
        total = total + part
    return total


def solve3(nu, theta):
    a = [[nu[r + c + 1] + theta * nu[r + c] for c in range(3)] for r in range(3)]
    l10, l20 = a[1][0] / a[0][0], a[2][0] / a[0][0]
    d1 = a[1][1] - l10 * a[1][0]
    e = a[2][1] - l20 * a[1][0]
    l21 = e / d1
    d2 = a[2][2] - l20 * a[2][0] - l21 * e
    z0 = nu[0]
    z1 = nu[1] - l10 * z0
    z2 = nu[2] - l20 * z0 - l21 * z1
    y2 = z2 / d2
    y1 = z1 / d1 - l21 * y2
    return z0 / a[0][0] - l10 * y1 - l20 * y2, y1, y2


def unpack(v_ref, exp_ref, out_ref):
    rows, four, total, modes = v_ref.shape
    x = jnp.concatenate([v_ref[j].reshape(four * total, modes) for j in range(rows)], axis=1)
    full = sum(dot(part, exp_ref[...], TN) for part in split2(x))
    out_ref[...] = full.reshape(out_ref.shape)


def expand_table(total):
    out = np.zeros((4 * total, 5 * total), np.float32)
    for e in range(total):
        for i in range(5):
            out[(i % 4) * total + (e + i // 4) % total, 5 * e + i] = 1.0
    return out.astype(bf16)


def segment(
    dims, x_ref, perm_ref, tag_ref, inv_hbm, fwd_hbm, exp_hbm, out_ref,
    inv, fwd, expand, w0, w1, w2, d_ref, dh, recv, hrecv, below, above, fld, halo, edge, carry,
    r_ref, h_ref, tsend, zlo, zhi, tjoin, trecv, c_ref, v0, v1, v2, lo, hi, part, parts,
    table_sem, s1, r1, sh, rh, s2, r2, sz, rz, s3, r3, s6, r6, s4, r4, s5, r5,
):
    span, planes, chunks, elems = dims
    modes, bl = x_ref.shape[1], 5 * elems
    sr, ab = 5 * bl, 8 * elems
    me, mp = lax.axis_index("span"), lax.axis_index("plane")
    first, last = mp == 0, mp == planes - 1
    inner, beyond = mp > 0, mp < planes - 1
    up, down = {"plane": lax.rem(mp + 1, planes)}, {"plane": lax.rem(mp + planes - 1, planes)}

    def remote(src, dst, send, recv_sem, device):
        return pltpu.make_async_remote_copy(
            src_ref=src, dst_ref=dst, send_sem=send, recv_sem=recv_sem,
            device_id=device, device_id_type=pl.DeviceIdType.MESH,
        )

    def peer(d):
        return lax.rem(me + d, span)

    barrier = pltpu.get_barrier_semaphore()
    for axis, here, count in (("span", me, span), ("plane", mp, planes)):
        for d in range(1, count):
            pl.semaphore_signal(
                barrier, inc=1, device_id={axis: lax.rem(here + d, count)},
                device_id_type=pl.DeviceIdType.MESH,
            )
    tables = [
        pltpu.make_async_copy(inv_hbm, inv, table_sem.at[0]),
        pltpu.make_async_copy(fwd_hbm, fwd, table_sem.at[1]),
        pltpu.make_async_copy(exp_hbm, expand, table_sem.at[2]),
    ]
    for copy in tables:
        copy.start()

    def to_span(s, start):
        off = lax.rem(s - me + span, span)
        pl.when(off > 0)(lambda: start(off - 1))

    def state_copy(k, s, n):
        src = d_ref.at[s * chunks + k]
        return remote(src, recv.at[k, me], s1.at[k, n], r1.at[k, n], {"span": s})

    def halo_copy(s, n):
        return remote(dh.at[s], hrecv.at[me], sh.at[n], rh.at[n], {"span": s})

    def row_copies(k):
        a = remote(recv.at[k, :, 4 * bl : 5 * bl, :], below.at[k], s2.at[k, 0], r2.at[k, 0], up)
        b = remote(recv.at[k, :, 0:bl, :], above.at[k], s2.at[k, 1], r2.at[k, 1], down)
        return a, b

    def shared_copies(k):
        src = tsend.at[k, :, 0 : ab + 8, :]
        a = remote(src, zlo.at[k], sz.at[k, 0], rz.at[k, 0], up)
        b = remote(src, zhi.at[k], sz.at[k, 1], rz.at[k, 1], down)
        return a, b

    def inner_copy(k, s, n):
        rows = slice(ab + 8, 20 * elems + 8)
        src, dst = tsend.at[k, s, rows, :], trecv.at[k, me, rows, :]
        return remote(src, dst, s3.at[k, n], r3.at[k, n], {"span": s})

    def outer_copy(k, s, n):
        rows = slice(0, ab + 8 if k == chunks - 1 else ab)
        src, dst = tjoin.at[k, s, rows, :], trecv.at[k, me, rows, :]
        return remote(src, dst, s6.at[k, n], r6.at[k, n], {"span": s})

    def join_copies(n):
        a = remote(c_ref.at[4], lo.at[n], s4.at[n, 0], r4.at[n, 0], up)
        b = remote(c_ref.at[0], hi.at[n], s4.at[n, 1], r4.at[n, 1], down)
        return a, b

    def part_copy(d):
        to = {"plane": lax.rem(mp + d, planes)}
        return remote(part, parts.at[mp], s5.at[d - 1], r5.at[d - 1], to)

    def tags(k):
        total = tag_ref.shape[1]
        element = lax.broadcasted_iota(jnp.int32, (elems, total), 0) + (me * chunks + k) * elems
        lane = lax.broadcasted_iota(jnp.int32, (elems, total), 1)
        column = jnp.sum(jnp.where(element == lane, tag_ref[...], 0), axis=1, keepdims=True)
        return jnp.concatenate([column] * 5, axis=0)

    def start_pair(pair):
        pl.when(beyond)(pair[0].start)
        pl.when(inner)(pair[1].start)

    def wait_sent(pair):
        pl.when(beyond)(pair[0].wait_send)
        pl.when(inner)(pair[1].wait_send)

    def wait_got(pair):
        pl.when(inner)(pair[0].wait_recv)
        pl.when(beyond)(pair[1].wait_recv)

    def ready(s):
        if s == 0:
            pl.semaphore_wait(barrier, span + planes - 2)
        to_span(s, lambda n: state_copy(0, s, n).start())

    pack(x_ref, perm_ref, d_ref, dh, span, chunks, elems, ready)
    for s in range(span):
        to_span(s, lambda n: halo_copy(s, n).start())
    for k in range(1, chunks):
        for s in range(span):
            to_span(s, lambda n: state_copy(k, s, n).start())
    column_load(d_ref, c_ref, elems, (0, 4))
    start_pair(join_copies(0))
    for k in range(chunks):
        recv[k, me] = d_ref[me * chunks + k]
    hrecv[me] = dh[me]

    @pl.when(first)
    def _():
        below[...] = jnp.zeros_like(below)
        zlo[...] = jnp.zeros_like(zlo)
        lo[...] = jnp.zeros_like(lo)

    @pl.when(last)
    def _():
        above[...] = jnp.zeros_like(above)
        zhi[...] = jnp.zeros_like(zhi)
        hi[...] = jnp.zeros_like(hi)

    column_load(d_ref, c_ref, elems, (1, 2, 3))
    join_rows(c_ref, None, None, None, None, v0, (1, 2, 3))

    def send_shared(k):
        wait_got(shared_copies(k))
        half = 4 * elems
        row = lax.broadcasted_iota(jnp.int32, (8, modes), 0)
        for s in range(span):
            tjoin[k, s, 0:half] = tsend[k, s, 0:half] + zlo[k, s, half:ab]
            tjoin[k, s, half:ab] = tsend[k, s, half:ab] + zhi[k, s, 0:half]
            if k == chunks - 1:
                ends = tsend[k, s, ab : ab + 8]
                ends = ends + jnp.where(row == 0, zlo[k, s, ab + 1 : ab + 2], 0.0)
                ends = ends + jnp.where(row == 1, zhi[k, s, ab : ab + 1], 0.0)
                tjoin[k, s, ab : ab + 8] = ends
            to_span(s, lambda n: outer_copy(k, s, n).start())
        rows = slice(0, ab + 8 if k == chunks - 1 else ab)
        trecv[k, me, rows] = tjoin[k, me, rows]

    for k in range(chunks):
        for d in range(1, span):
            state_copy(k, peer(d), d - 1).wait_recv()
        start_pair(row_copies(k))
        if k == 0:
            for copy in tables:
                copy.wait()
        to_planes([recv.at[k]], inv, fld, 0)
        if k == 0:
            for d in range(1, span):
                halo_copy(peer(d), d - 1).wait_recv()
            to_planes([hrecv], inv, halo, 0)
        else:
            send_shared(k - 1)
        wait_got(row_copies(k))
        to_planes([below.at[k], above.at[k]], inv, fld, sr)
        outer_rows(fld, tags(k), elems, first, last)
        pointwise(fld, halo, edge, carry, r_ref, h_ref, elems, k, chunks)

        def send_inner(s):
            to_span(s, lambda n: inner_copy(k, s, n).start())

        spectral(r_ref, h_ref, fwd, tsend.at[k], send_inner)
        start_pair(shared_copies(k))
        rows = slice(ab + 8, 20 * elems + 8)
        trecv[k, me, rows] = tsend[k, me, rows]
        if k == 0:
            wait_got(join_copies(0))
            join_rows(c_ref, lo.at[0], hi.at[0], None, None, v0, (0, 4))
            wait_sent(join_copies(0))
    send_shared(chunks - 1)

    for k in range(chunks):
        for d in range(1, span):
            inner_copy(k, peer(d), d - 1).wait_recv()
            outer_copy(k, peer(d), d - 1).wait_recv()
        add_tendency(v0, trecv, elems, k, chunks)
    add_ends(v0, trecv, elems, chunks)

    ids = me * modes + lax.broadcasted_iota(jnp.int32, (1, modes), 1)
    wave = lax.shift_right_logical(ids, 1).astype(f32) / KMODES
    shift = 1.0 + STIFF * wave * wave
    theta = 0.6 + 0.254 * (shift - 1.0)
    sums = []
    prev = None
    for n, (v, w) in enumerate(((v0, w0), (v1, w1), (v2, w2))):
        if n > 0:
            join = functools.partial(join_rows, c_ref, lo.at[n], hi.at[n], prev, theta, v)
            join((1, 2, 3))
            stretch(v, c_ref, (1, 2, 3))
            wait_got(join_copies(n))
            join((0, 4))
            wait_sent(join_copies(n))
        stretch(v, c_ref, (0, 4))
        outer = image(v, c_ref, shift, (0, 4))
        if n < 2:
            start_pair(join_copies(n + 1))
        if n == 0:
            stretch(v, c_ref, (1, 2, 3))
        sums.append(squares(v, first, last, range(5)))
        sums.append(outer + image(v, c_ref, shift, (1, 2, 3)))
        if n < 2:
            unpack(v, expand, w)
        prev = v
    rows = [jnp.sum(t, axis=0, keepdims=True) for t in sums]
    part[...] = jnp.concatenate(rows + [jnp.zeros_like(rows[0])] * 2, axis=0)
    for d in range(1, planes):
        part_copy(d).start()
    parts[mp] = part[...]
    unpack(v2, expand, w2)
    for d in range(1, planes):
        part_copy(d).wait_recv()
    got = jnp.sum(parts[...], axis=0)
    n0, h0, n2, h2, n4, h4 = [got[k : k + 1] for k in range(6)]
    nu = [n0, h0 - theta * n0, n2, h2 - theta * n2, n4, h4 - theta * n4]
    y = solve3(nu, theta)
    y = jnp.concatenate(list(y) + [jnp.zeros_like(y[0])] * 5, axis=0).T
    y0, y1, y2 = y[:, 0:1], y[:, 1:2], y[:, 2:3]
    for j in range(5):
        out_ref[j] = y0 * w0[j] + y1 * w1[j] + y2 * w2[j]
    for d in range(1, span):
        halo_copy(peer(d), d - 1).wait_send()
    for k in range(chunks):
        for d in range(1, span):
            state_copy(k, peer(d), d - 1).wait_send()
            inner_copy(k, peer(d), d - 1).wait_send()
            outer_copy(k, peer(d), d - 1).wait_send()
        wait_sent(row_copies(k))
        wait_sent(shared_copies(k))
    for d in range(1, planes):
        part_copy(d).wait_send()


def place(x_hbm, out_hbm, sems):
    copies = [
        pltpu.make_async_copy(x_hbm.at[j], out_hbm.at[j], sems.at[j])
        for j in range(x_hbm.shape[0])
    ]
    for copy in copies:
        copy.start()
    for copy in copies:
        copy.wait()


def shape(*dims):
    return jax.ShapeDtypeStruct(dims, f32)


def on_device(state, wall_tag):
    modes, rows, cols = state.shape
    assert rows == 5
    span, planes = lax.axis_size("span"), lax.axis_size("plane")
    total = cols // 5
    mine = total // span
    chunks = mine // 8
    elems = mine // chunks
    bl = 5 * elems
    sr, tr, shared = 5 * bl, 20 * elems + 8, 8 * elems + 8
    halos = -(-5 * (chunks + 1) // 8) * 8
    inverse, inner, outer = basis_tables()
    inv = jnp.asarray(np.stack(halves(inverse)))
    fwd = jnp.asarray(np.stack(halves(inner) + halves(outer)))
    perm = jnp.asarray(perm_tables(span, chunks, elems))
    expand = jnp.asarray(expand_table(total))
    vmem = pl.BlockSpec(memory_space=pltpu.VMEM)
    hbm = pl.BlockSpec(memory_space=pl.ANY)
    buf = lambda *d: pltpu.VMEM(d, f32)
    dma = lambda *d: pltpu.SemaphoreType.DMA(d)
    joined = buf(5, 4, total, modes)
    halo = buf(3, 4, total, modes)

    out = pl.pallas_call(
        functools.partial(segment, (span, planes, chunks, elems)),
        out_shape=shape(5, modes, cols),
        in_specs=[vmem] * 3 + [hbm] * 3,
        out_specs=vmem,
        scratch_shapes=[
            pltpu.VMEM(inv.shape, bf16),
            pltpu.VMEM(fwd.shape, bf16),
            pltpu.VMEM(expand.shape, bf16),
            buf(5, modes, cols), buf(5, modes, cols), buf(5, modes, cols),
            buf(span * chunks, sr, modes),
            buf(span, halos, modes),
            buf(chunks, span, sr, modes),
            buf(span, halos, modes),
            buf(chunks, span, bl, modes),
            buf(chunks, span, bl, modes),
            buf(sr + 2 * bl, PLANES),
            buf(halos, PLANES),
            buf(8, PLANES),
            buf(16, PLANES),
            buf(tr, PLANES),
            buf(tr, PLANES),
            buf(chunks, span, tr, modes),
            buf(chunks, span, shared, modes),
            buf(chunks, span, shared, modes),
            buf(chunks, span, shared, modes),
            buf(chunks, span, tr, modes),
            joined, joined, joined, joined, halo, halo,
            buf(8, modes),
            buf(planes, 8, modes),
            dma(3),
            dma(chunks, span - 1), dma(chunks, span - 1),
            dma(span - 1), dma(span - 1),
            dma(chunks, 2), dma(chunks, 2),
            dma(chunks, 2), dma(chunks, 2),
            dma(chunks, span - 1), dma(chunks, span - 1),
            dma(chunks, span - 1), dma(chunks, span - 1),
            dma(3, 2), dma(3, 2),
            dma(planes - 1), dma(planes - 1),
        ],
        compiler_params=pltpu.CompilerParams(
            vmem_limit_bytes=VMEM_LIMIT, collective_id=0, has_side_effects=True
        ),
    )(state.transpose(1, 0, 2), perm, wall_tag.reshape(1, total), inv, fwd, expand)
    out = pl.pallas_call(
        place,
        out_shape=shape(5, modes, cols),
        in_specs=[hbm],
        out_specs=hbm,
        scratch_shapes=[dma(5)],
    )(out)
    return out.transpose(1, 0, 2)


def solution(mesh):
    spec = P("span", "plane", None)
    return jax.shard_map(
        on_device, mesh=mesh, in_specs=(spec, P()), out_specs=spec, check_vma=False
    )
```

```python
import functools
import math

import jax
import jax.numpy as jnp
import numpy as np
from jax import lax
from jax.experimental import pallas as pl
from jax.experimental.pallas import tpu as pltpu
from jax.sharding import PartitionSpec as P

KMODES = 256
PLANES = 768
STEP = 0.03
VISCOUS = 0.05
STIFF = 4.0

f32 = jnp.float32
bf16 = jnp.bfloat16
NT = (((1,), (1,)), ((), ()))
NN = (((1,), (0,)), ((), ()))
TN = (((0,), (0,)), ((), ()))
VMEM_LIMIT = 56 * 1024 * 1024


def gll_tables():
    x = np.array([-1.0, -math.sqrt(3.0 / 7.0), 0.0, math.sqrt(3.0 / 7.0), 1.0])
    w = np.array([0.1, 49.0 / 90.0, 32.0 / 45.0, 49.0 / 90.0, 0.1])
    q = x * x
    leg = (35.0 * q * q - 30.0 * q + 3.0) / 8.0
    eye = np.eye(5)
    d = np.where(eye > 0, 0.0, leg[:, None] / leg[None, :] / (x[:, None] - x[None, :] + eye))
    d[0, 0], d[4, 4] = -5.0, 5.0
    return d, w, d.T @ (w[:, None] * d)


DIFF, WEIGHT, KMAT = gll_tables()


def halves(table):
    high = table.astype(np.float32).astype(bf16)
    low = (table.astype(np.float32) - high.astype(np.float32)).astype(bf16)
    return high, low


def basis_tables():
    k, p = np.arange(KMODES), np.arange(PLANES)
    angle = 2.0 * math.pi * (p[:, None] * k[None, :] % PLANES) / PLANES
    cos, sin = np.cos(angle), np.sin(angle)
    inverse = np.stack([cos, sin], 2).reshape(PLANES, 2 * KMODES).T / math.sqrt(KMODES)
    factor = np.where(k == 0, 1.0, 2.0) * (math.sqrt(KMODES) / PLANES) * STEP
    ratio = k / KMODES
    inner = np.stack([cos * factor, sin * factor], 2).reshape(PLANES, 2 * KMODES)
    span = np.stack([-ratio * sin * factor, ratio * cos * factor], 2).reshape(PLANES, 2 * KMODES)
    return inverse, inner, span


def split2(x):
    high = x.astype(bf16)
    return high, (x - high.astype(f32)).astype(bf16)


def dot(a, b, dims=NN):
    return lax.dot_general(a, b, dims, preferred_element_type=f32)


def along(mat, a, flip):
    s1, d1, s2, d2, m = a[0] + a[4], a[0] - a[4], a[1] + a[3], a[1] - a[3], a[2]
    out = [None] * 5
    for r in (0, 1):
        e = [0.5 * (mat[r][b] + mat[r][4 - b]) for b in (0, 1)]
        o = [0.5 * (mat[r][b] - mat[r][4 - b]) for b in (0, 1)]
        even = float(e[0]) * s1 + float(e[1]) * s2 + float(mat[r][2]) * m
        odd = float(o[0]) * d1 + float(o[1]) * d2
        out[r] = even + odd
        out[4 - r] = even - odd if flip > 0 else odd - even
    if flip > 0:
        out[2] = float(mat[2][0]) * s1 + float(mat[2][1]) * s2 + float(mat[2][2]) * m
    else:
        out[2] = float(mat[2][0]) * d1 + float(mat[2][1]) * d2
    return out


def two_point10(a, b, qa, qb):
    speed = jnp.maximum(jnp.abs(a), jnp.abs(b))
    return (qa + a * b + qb) * (10.0 / 6.0) - 5.0 * speed * (b - a)


def roll(x, by):
    return pltpu.roll(x, by % x.shape[0], 0)


def pack(x_ref, perm_ref, d_ref, halo_ref, span, chunks, elems):
    rows, modes, cols = x_ref.shape
    block = 5 * elems
    wide = block * chunks
    blocks = span * chunks
    parts = split2(x_ref[...].reshape(rows * modes, cols))
    for s in range(span):
        lo = wide * s // 128 * 128
        hi = -(-wide * (s + 1) // 128) * 128
        perm = perm_ref[s, :, : hi - lo]
        got = sum(dot(perm, part[:, lo:hi], NT) for part in parts)
        for k in range(chunks):
            for j in range(rows):
                d_ref[s * chunks + k, block * j : block * (j + 1), :] = got[
                    block * k : block * (k + 1), modes * j : modes * (j + 1)
                ]
    for s in range(span):
        left = (s * chunks - 1) % blocks
        for j in range(rows):
            last = block * j + block - 1
            halo_ref[s, j : j + 1, :] = d_ref[left, last : last + 1, :]
            for k in range(chunks):
                right = (s * chunks + k + 1) % blocks
                at = rows * (k + 1) + j
                halo_ref[s, at : at + 1, :] = d_ref[right, block * j : block * j + 1, :]
        used = rows * (chunks + 1)
        halo_ref[s, used:, :] = jnp.zeros((halo_ref.shape[1] - used, modes), f32)


def perm_tables(span, chunks, elems):
    wide = 5 * elems * chunks
    width = max(-(-wide * (s + 1) // 128) * 128 - wide * s // 128 * 128 for s in range(span))
    perm = np.zeros((span, wide, width), np.float32)
    for s in range(span):
        lo = wide * s // 128 * 128
        for k in range(chunks):
            for i in range(5):
                for e in range(elems):
                    row = (k * 5 + i) * elems + e
                    perm[s, row, wide * s + 5 * (k * elems + e) + i - lo] = 1.0
    return perm.astype(bf16)


def to_planes(parts, inv_ref, fld_ref, lo):
    x = jnp.concatenate(
        [jnp.concatenate([p[s] for s in range(p.shape[0])], axis=1) for p in parts], axis=0
    )
    high, low = split2(x)
    for n in range(PLANES // 256):
        at = slice(n * 256, (n + 1) * 256)
        bh, bl = inv_ref[0, :, at], inv_ref[1, :, at]
        fld_ref[lo : lo + x.shape[0], at] = dot(high, bh) + dot(high, bl) + dot(low, bh)


def outer_rows(fld_ref, tag, elems, first, last):
    block = 5 * elems
    sr = 5 * block

    @pl.when(first)
    def _():
        own = fld_ref[0:block, :]
        fld_ref[sr : sr + block, :] = jnp.where(tag == 1, -own, own)

    @pl.when(last)
    def _():
        fld_ref[sr + block : sr + 2 * block, :] = fld_ref[4 * block : 5 * block, :]


def pointwise(fld_ref, halo_ref, edge_ref, carry_ref, r_ref, h_ref, elems, k, chunks):
    block = 5 * elems
    sr = 5 * block
    lane = 128
    place = {0: 0, 4: 4 * elems}
    for j in (1, 2, 3):
        place[j] = 4 * elems * (j + 1) + 8
    third = DIFF * (-1.0 / 3.0)

    def body(n, _):
        at = pl.ds(pl.multiple_of(n * lane, lane), lane)
        row = lax.broadcasted_iota(jnp.int32, (elems, lane), 0)

        def load(base):
            return fld_ref[base : base + elems, at]

        u = [[load(block * j + elems * i) for i in range(5)] for j in range(5)]
        q = [[v * v for v in r] for r in u]
        rhs = [[None] * 5 for _ in range(5)]
        for j in range(5):
            du = along(third, u[j], -1)
            dq = along(third, q[j], -1)
            for i in range(5):
                rhs[j][i] = dq[i] + u[j][i] * du[i]
            hl = halo_ref[j : j + 1, at] if k == 0 else edge_ref[j : j + 1, at]
            hr = halo_ref[5 * (k + 1) + j : 5 * (k + 1) + j + 1, at]
            edge_ref[j : j + 1, at] = u[j][4][elems - 1 : elems, :]
            left = jnp.where(row == 0, hl, roll(u[j][4], 1))
            right = jnp.where(row == elems - 1, hr, roll(u[j][0], -1))
            rhs[j][0] += two_point10(left, u[j][0], left * left, q[j][0]) - 5.0 * q[j][0]
            rhs[j][4] -= two_point10(u[j][4], right, q[j][4], right * right) - 5.0 * q[j][4]
        for i in range(5):
            ui, qi = [u[j][i] for j in range(5)], [q[j][i] for j in range(5)]
            du = along(third, ui, -1)
            dq = along(third, qi, -1)
            for j in range(5):
                rhs[j][i] += dq[j] + ui[j] * du[j]
            lower = load(sr + elems * i)
            upper = load(sr + block + elems * i)
            rhs[0][i] += two_point10(lower, ui[0], lower * lower, qi[0]) - 5.0 * qi[0]
            rhs[4][i] -= two_point10(ui[4], upper, qi[4], upper * upper) - 5.0 * qi[4]
        for ref, val, scale, base in ((r_ref, rhs, None, 0), (h_ref, q, 0.5, 5)):
            for n, j in enumerate((0, 4, 1, 2, 3)):
                a = val[j] if scale is None else [scale * v for v in val[j]]
                kept = 0.0 if k == 0 else carry_ref[base + j : base + j + 1, at]
                ref[place[j] : place[j] + elems, at] = a[0] + jnp.where(
                    row == 0, kept, roll(a[4], 1)
                )
                for i in (1, 2, 3):
                    to = place[j] + elems * i
                    ref[to : to + elems, at] = a[i]
                tail = a[4][elems - 1 : elems, :]
                if k == chunks - 1:
                    ref[8 * elems + n : 8 * elems + n + 1, at] = tail
                else:
                    carry_ref[base + j : base + j + 1, at] = tail
            if k == chunks - 1:
                ref[8 * elems + 5 : 8 * elems + 8, at] = jnp.zeros((3, lane), f32)
            else:
                ref[8 * elems : 8 * elems + 8, at] = jnp.zeros((8, lane), f32)
        return 0

    lax.fori_loop(0, PLANES // lane, body, 0)


def spectral(r_ref, h_ref, fwd_ref, t_ref):
    span, _, modes = t_ref.shape
    rh, rl = split2(r_ref[...])
    hh, hl = split2(h_ref[...])
    step = max(modes, 256)
    for n in range(span * modes // step):
        at = slice(n * step, (n + 1) * step)
        a, b = fwd_ref[0, :, at], fwd_ref[1, :, at]
        c, d = fwd_ref[2, :, at], fwd_ref[3, :, at]
        t = dot(rh, a) + dot(rl, a) + dot(rh, b) + dot(hh, c) + dot(hl, c) + dot(hh, d)
        for k in range(step // modes):
            s = n * (step // modes) + k
            t_ref[s] = t[:, modes * k : modes * (k + 1)]


def column_load(d_ref, c_ref, elems, js):
    blocks, _, modes = d_ref.shape
    block = 5 * elems
    row = lax.broadcasted_iota(jnp.int32, (elems, modes), 0)
    for j in js:
        for b in range(blocks):
            left = (b - 1) % blocks
            for i in range(4):
                at = block * j + elems * i
                val = d_ref[b, at : at + elems, :]
                if i == 0:
                    at4 = block * j + 4 * elems
                    edge = d_ref[left, at4 + elems - 1 : at4 + elems, :]
                    val += jnp.where(row == 0, edge, roll(d_ref[b, at4 : at4 + elems, :], 1))
                c_ref[j, i, elems * b : elems * (b + 1), :] = val * float(WEIGHT[j] * WEIGHT[i])


def add_tendency(v_ref, t_ref, elems, k, chunks):
    span = t_ref.shape[1]
    for j in range(5):
        base = {0: 0, 4: 4 * elems}.get(j, 4 * elems * (j + 1) + 8)
        for s in range(span):
            at = slice(elems * (s * chunks + k), elems * (s * chunks + k + 1))
            for i in range(4):
                part = t_ref[k, s, base + elems * i : base + elems * (i + 1), :]
                v_ref[j, i, at, :] += part * float(WEIGHT[j] * WEIGHT[i])


def add_ends(v_ref, t_ref, elems, chunks):
    span = t_ref.shape[1]
    for n, j in enumerate((0, 4, 1, 2, 3)):
        for s in range(span):
            end = t_ref[chunks - 1, (s - 1) % span, 8 * elems + n : 8 * elems + n + 1, :]
            at = elems * s * chunks
            v_ref[j, 0, at : at + 1, :] += end * float(WEIGHT[j] * WEIGHT[0])


def fold(x):
    return jnp.sum(x.reshape(x.shape[0] // 8, 8, x.shape[1]), axis=0)


COLW = [2.0 * WEIGHT[0], WEIGHT[1], WEIGHT[2], WEIGHT[3]]


def stretch(v_ref, out_ref, js):
    for j in js:
        a = [v_ref[j, i] for i in range(4)]
        a.append(roll(a[0], -1))
        kx = along(KMAT * (VISCOUS * WEIGHT[j]), a, 1)
        kx[0] = kx[0] + roll(kx[4], 1)
        for i in range(4):
            out_ref[j, i] = kx[i]


def image(v_ref, out_ref, shift, js):
    total = 0.0
    for i in range(4):
        a = [v_ref[j, i] for j in range(5)]
        ky = along(KMAT * (VISCOUS * COLW[i]), a, 1)
        for j in js:
            val = out_ref[j, i] + ky[j] + (shift * float(WEIGHT[j] * COLW[i])) * a[j]
            out_ref[j, i] = val
            total = total + fold(val * a[j])
    return total


def join_rows(c_ref, lo, hi, prev, theta, v_ref, js):
    for j in js:
        for i in range(4):
            val = c_ref[j, i]
            if j == 0:
                val = val + lo[i]
            if j == 4:
                val = val + hi[i]
            if prev is not None:
                val = val - theta * prev[j, i]
            v_ref[j, i] = val


def squares(v_ref, first, last, js):
    total = 0.0
    for j in js:
        part = sum(fold(v_ref[j, i] * v_ref[j, i]) for i in range(4))
        if j == 0:
            part = part * jnp.where(first, 1.0, 0.5)
        if j == 4:
            part = part * jnp.where(last, 1.0, 0.5)
        total = total + part
    return total


def solve3(nu, theta):
    a = [[nu[r + c + 1] + theta * nu[r + c] for c in range(3)] for r in range(3)]
    l10, l20 = a[1][0] / a[0][0], a[2][0] / a[0][0]
    d1 = a[1][1] - l10 * a[1][0]
    e = a[2][1] - l20 * a[1][0]
    l21 = e / d1
    d2 = a[2][2] - l20 * a[2][0] - l21 * e
    z0 = nu[0]
    z1 = nu[1] - l10 * z0
    z2 = nu[2] - l20 * z0 - l21 * z1
    y2 = z2 / d2
    y1 = z1 / d1 - l21 * y2
    return z0 / a[0][0] - l10 * y1 - l20 * y2, y1, y2


def unpack(v_ref, exp_ref, out_ref):
    rows, four, total, modes = v_ref.shape
    x = jnp.concatenate([v_ref[j].reshape(four * total, modes) for j in range(rows)], axis=1)
    full = sum(dot(part, exp_ref[...], TN) for part in split2(x))
    out_ref[...] = full.reshape(out_ref.shape)


def expand_table(total):
    out = np.zeros((4 * total, 5 * total), np.float32)
    for e in range(total):
        for i in range(5):
            out[(i % 4) * total + (e + i // 4) % total, 5 * e + i] = 1.0
    return out.astype(bf16)


def segment(
    dims, x_ref, perm_ref, tag_ref, inv_hbm, fwd_hbm, exp_hbm, out_ref,
    inv, fwd, expand, w0, w1, w2, d_ref, dh, recv, hrecv, below, above, fld, halo, edge, carry,
    r_ref, h_ref, tsend, zlo, zhi, tjoin, trecv, c_ref, v0, v1, v2, lo, hi, part, parts,
    table_sem, s1, r1, sh, rh, s2, r2, sz, rz, s3, r3, s6, r6, s4, r4, s5, r5,
):
    span, planes, chunks, elems = dims
    modes, bl = x_ref.shape[1], 5 * elems
    sr, ab = 5 * bl, 8 * elems
    me, mp = lax.axis_index("span"), lax.axis_index("plane")
    first, last = mp == 0, mp == planes - 1
    inner, beyond = mp > 0, mp < planes - 1
    up, down = {"plane": lax.rem(mp + 1, planes)}, {"plane": lax.rem(mp + planes - 1, planes)}

    def remote(src, dst, send, recv_sem, device):
        return pltpu.make_async_remote_copy(
            src_ref=src, dst_ref=dst, send_sem=send, recv_sem=recv_sem,
            device_id=device, device_id_type=pl.DeviceIdType.MESH,
        )

    def peer(d):
        return lax.rem(me + d, span)

    barrier = pltpu.get_barrier_semaphore()
    for axis, here, count in (("span", me, span), ("plane", mp, planes)):
        for d in range(1, count):
            pl.semaphore_signal(
                barrier, inc=1, device_id={axis: lax.rem(here + d, count)},
                device_id_type=pl.DeviceIdType.MESH,
            )
    tables = [
        pltpu.make_async_copy(inv_hbm, inv, table_sem.at[0]),
        pltpu.make_async_copy(fwd_hbm, fwd, table_sem.at[1]),
        pltpu.make_async_copy(exp_hbm, expand, table_sem.at[2]),
    ]
    for copy in tables:
        copy.start()

    def to_peers(start):
        for i in range(span - 1):
            d = 1 + lax.rem(i + lax.rem(mp, 2) * (span // 2 - 1), span - 1)
            start(peer(d), d - 1)

    def state_copy(k, s, n):
        src = d_ref.at[s * chunks + k]
        return remote(src, recv.at[k, me], s1.at[k, n], r1.at[k, n], {"span": s})

    def halo_copy(s, n):
        return remote(dh.at[s], hrecv.at[me], sh.at[n], rh.at[n], {"span": s})

    def row_copies(k):
        a = remote(recv.at[k, :, 4 * bl : 5 * bl, :], below.at[k], s2.at[k, 0], r2.at[k, 0], up)
        b = remote(recv.at[k, :, 0:bl, :], above.at[k], s2.at[k, 1], r2.at[k, 1], down)
        return a, b

    def shared_copies(k):
        src = tsend.at[k, :, 0 : ab + 8, :]
        a = remote(src, zlo.at[k], sz.at[k, 0], rz.at[k, 0], up)
        b = remote(src, zhi.at[k], sz.at[k, 1], rz.at[k, 1], down)
        return a, b

    def inner_copy(k, s, n):
        rows = slice(ab + 8, 20 * elems + 8)
        src, dst = tsend.at[k, s, rows, :], trecv.at[k, me, rows, :]
        return remote(src, dst, s3.at[k, n], r3.at[k, n], {"span": s})

    def outer_copy(k, s, n):
        rows = slice(0, ab + 8 if k == chunks - 1 else ab)
        src, dst = tjoin.at[k, s, rows, :], trecv.at[k, me, rows, :]
        return remote(src, dst, s6.at[k, n], r6.at[k, n], {"span": s})

    def join_copies(n):
        a = remote(c_ref.at[4], lo.at[n], s4.at[n, 0], r4.at[n, 0], up)
        b = remote(c_ref.at[0], hi.at[n], s4.at[n, 1], r4.at[n, 1], down)
        return a, b

    def part_copy(d):
        to = {"plane": lax.rem(mp + d, planes)}
        return remote(part, parts.at[mp], s5.at[d - 1], r5.at[d - 1], to)

    def tags(k):
        total = tag_ref.shape[1]
        element = lax.broadcasted_iota(jnp.int32, (elems, total), 0) + (me * chunks + k) * elems
        lane = lax.broadcasted_iota(jnp.int32, (elems, total), 1)
        column = jnp.sum(jnp.where(element == lane, tag_ref[...], 0), axis=1, keepdims=True)
        return jnp.concatenate([column] * 5, axis=0)

    def start_pair(pair):
        pl.when(beyond)(pair[0].start)
        pl.when(inner)(pair[1].start)

    def wait_sent(pair):
        pl.when(beyond)(pair[0].wait_send)
        pl.when(inner)(pair[1].wait_send)

    def wait_got(pair):
        pl.when(inner)(pair[0].wait_recv)
        pl.when(beyond)(pair[1].wait_recv)

    pack(x_ref, perm_ref, d_ref, dh, span, chunks, elems)
    pl.semaphore_wait(barrier, span + planes - 2)
    to_peers(lambda s, n: state_copy(0, s, n).start())
    to_peers(lambda s, n: halo_copy(s, n).start())
    for k in range(chunks):
        recv[k, me] = d_ref[me * chunks + k]
    hrecv[me] = dh[me]

    @pl.when(first)
    def _():
        below[...] = jnp.zeros_like(below)
        zlo[...] = jnp.zeros_like(zlo)
        lo[...] = jnp.zeros_like(lo)

    @pl.when(last)
    def _():
        above[...] = jnp.zeros_like(above)
        zhi[...] = jnp.zeros_like(zhi)
        hi[...] = jnp.zeros_like(hi)

    column_load(d_ref, c_ref, elems, range(5))
    join_rows(c_ref, None, None, None, None, v0, (1, 2, 3))

    def send_shared(k):
        wait_got(shared_copies(k))
        half = 4 * elems
        row = lax.broadcasted_iota(jnp.int32, (8, modes), 0)
        for s in range(span):
            tjoin[k, s, 0:half] = tsend[k, s, 0:half] + zlo[k, s, half:ab]
            tjoin[k, s, half:ab] = tsend[k, s, half:ab] + zhi[k, s, 0:half]
            if k == chunks - 1:
                ends = tsend[k, s, ab : ab + 8]
                ends = ends + jnp.where(row == 0, zlo[k, s, ab + 1 : ab + 2], 0.0)
                ends = ends + jnp.where(row == 1, zhi[k, s, ab : ab + 1], 0.0)
                tjoin[k, s, ab : ab + 8] = ends
        to_peers(lambda s, n: outer_copy(k, s, n).start())
        rows = slice(0, ab + 8 if k == chunks - 1 else ab)
        trecv[k, me, rows] = tjoin[k, me, rows]

    for k in range(chunks):
        for d in range(1, span):
            state_copy(k, peer(d), d - 1).wait_recv()
        start_pair(row_copies(k))
        if k < chunks - 1:
            to_peers(lambda s, n: state_copy(k + 1, s, n).start())
        else:
            start_pair(join_copies(0))
        if k == 0:
            for copy in tables:
                copy.wait()
        to_planes([recv.at[k]], inv, fld, 0)
        if k == 0:
            for d in range(1, span):
                halo_copy(peer(d), d - 1).wait_recv()
            to_planes([hrecv], inv, halo, 0)
        else:
            send_shared(k - 1)
        wait_got(row_copies(k))
        to_planes([below.at[k], above.at[k]], inv, fld, sr)
        outer_rows(fld, tags(k), elems, first, last)
        pointwise(fld, halo, edge, carry, r_ref, h_ref, elems, k, chunks)

        spectral(r_ref, h_ref, fwd, tsend.at[k])
        start_pair(shared_copies(k))
        to_peers(lambda s, n: inner_copy(k, s, n).start())
        rows = slice(ab + 8, 20 * elems + 8)
        trecv[k, me, rows] = tsend[k, me, rows]
    send_shared(chunks - 1)
    wait_got(join_copies(0))
    join_rows(c_ref, lo.at[0], hi.at[0], None, None, v0, (0, 4))
    wait_sent(join_copies(0))

    for k in range(chunks):
        for d in range(1, span):
            inner_copy(k, peer(d), d - 1).wait_recv()
            outer_copy(k, peer(d), d - 1).wait_recv()
        add_tendency(v0, trecv, elems, k, chunks)
    add_ends(v0, trecv, elems, chunks)

    ids = me * modes + lax.broadcasted_iota(jnp.int32, (1, modes), 1)
    wave = lax.shift_right_logical(ids, 1).astype(f32) / KMODES
    shift = 1.0 + STIFF * wave * wave
    theta = 0.6 + 0.254 * (shift - 1.0)
    sums = []
    prev = None
    for n, (v, w) in enumerate(((v0, w0), (v1, w1), (v2, w2))):
        if n > 0:
            join = functools.partial(join_rows, c_ref, lo.at[n], hi.at[n], prev, theta, v)
            join((1, 2, 3))
            stretch(v, c_ref, (1, 2, 3))
            wait_got(join_copies(n))
            join((0, 4))
            wait_sent(join_copies(n))
        stretch(v, c_ref, (0, 4))
        outer = image(v, c_ref, shift, (0, 4))
        if n < 2:
            start_pair(join_copies(n + 1))
        if n == 0:
            stretch(v, c_ref, (1, 2, 3))
        sums.append(squares(v, first, last, range(5)))
        sums.append(outer + image(v, c_ref, shift, (1, 2, 3)))
        if n < 2:
            unpack(v, expand, w)
        prev = v
    rows = [jnp.sum(t, axis=0, keepdims=True) for t in sums]
    part[...] = jnp.concatenate(rows + [jnp.zeros_like(rows[0])] * 2, axis=0)
    for d in range(1, planes):
        part_copy(d).start()
    parts[mp] = part[...]
    unpack(v2, expand, w2)
    for d in range(1, planes):
        part_copy(d).wait_recv()
    got = jnp.sum(parts[...], axis=0)
    n0, h0, n2, h2, n4, h4 = [got[k : k + 1] for k in range(6)]
    nu = [n0, h0 - theta * n0, n2, h2 - theta * n2, n4, h4 - theta * n4]
    y = solve3(nu, theta)
    y = jnp.concatenate(list(y) + [jnp.zeros_like(y[0])] * 5, axis=0).T
    y0, y1, y2 = y[:, 0:1], y[:, 1:2], y[:, 2:3]
    for j in range(5):
        out_ref[j] = y0 * w0[j] + y1 * w1[j] + y2 * w2[j]
    for d in range(1, span):
        halo_copy(peer(d), d - 1).wait_send()
    for k in range(chunks):
        for d in range(1, span):
            state_copy(k, peer(d), d - 1).wait_send()
            inner_copy(k, peer(d), d - 1).wait_send()
            outer_copy(k, peer(d), d - 1).wait_send()
        wait_sent(row_copies(k))
        wait_sent(shared_copies(k))
    for d in range(1, planes):
        part_copy(d).wait_send()


def place(x_ref, out_ref):
    out_ref[...] = x_ref[...]


def shape(*dims):
    return jax.ShapeDtypeStruct(dims, f32)


def on_device(state, wall_tag):
    modes, rows, cols = state.shape
    assert rows == 5
    span, planes = lax.axis_size("span"), lax.axis_size("plane")
    total = cols // 5
    mine = total // span
    chunks = mine // 8
    elems = mine // chunks
    bl = 5 * elems
    sr, tr, shared = 5 * bl, 20 * elems + 8, 8 * elems + 8
    halos = -(-5 * (chunks + 1) // 8) * 8
    inverse, inner, outer = basis_tables()
    inv = jnp.asarray(np.stack(halves(inverse)))
    fwd = jnp.asarray(np.stack(halves(inner) + halves(outer)))
    perm = jnp.asarray(perm_tables(span, chunks, elems))
    expand = jnp.asarray(expand_table(total))
    vmem = pl.BlockSpec(memory_space=pltpu.VMEM)
    hbm = pl.BlockSpec(memory_space=pl.ANY)
    buf = lambda *d: pltpu.VMEM(d, f32)
    dma = lambda *d: pltpu.SemaphoreType.DMA(d)
    joined = buf(5, 4, total, modes)
    halo = buf(3, 4, total, modes)

    out = pl.pallas_call(
        functools.partial(segment, (span, planes, chunks, elems)),
        out_shape=shape(5, modes, cols),
        in_specs=[vmem] * 3 + [hbm] * 3,
        out_specs=vmem,
        scratch_shapes=[
            pltpu.VMEM(inv.shape, bf16),
            pltpu.VMEM(fwd.shape, bf16),
            pltpu.VMEM(expand.shape, bf16),
            buf(5, modes, cols), buf(5, modes, cols), buf(5, modes, cols),
            buf(span * chunks, sr, modes),
            buf(span, halos, modes),
            buf(chunks, span, sr, modes),
            buf(span, halos, modes),
            buf(chunks, span, bl, modes),
            buf(chunks, span, bl, modes),
            buf(sr + 2 * bl, PLANES),
            buf(halos, PLANES),
            buf(8, PLANES),
            buf(16, PLANES),
            buf(tr, PLANES),
            buf(tr, PLANES),
            buf(chunks, span, tr, modes),
            buf(chunks, span, shared, modes),
            buf(chunks, span, shared, modes),
            buf(chunks, span, shared, modes),
            buf(chunks, span, tr, modes),
            joined, joined, joined, joined, halo, halo,
            buf(8, modes),
            buf(planes, 8, modes),
            dma(3),
            dma(chunks, span - 1), dma(chunks, span - 1),
            dma(span - 1), dma(span - 1),
            dma(chunks, 2), dma(chunks, 2),
            dma(chunks, 2), dma(chunks, 2),
            dma(chunks, span - 1), dma(chunks, span - 1),
            dma(chunks, span - 1), dma(chunks, span - 1),
            dma(3, 2), dma(3, 2),
            dma(planes - 1), dma(planes - 1),
        ],
        compiler_params=pltpu.CompilerParams(
            vmem_limit_bytes=VMEM_LIMIT, collective_id=0, has_side_effects=True
        ),
    )(state.transpose(1, 0, 2), perm, wall_tag.reshape(1, total), inv, fwd, expand)
    out = pl.pallas_call(
        place,
        out_shape=shape(5, modes, cols),
        grid=(5,),
        in_specs=[pl.BlockSpec((1, modes, cols), lambda j: (j, 0, 0))],
        out_specs=pl.BlockSpec((1, modes, cols), lambda j: (j, 0, 0)),
    )(out)
    return out.transpose(1, 0, 2)


def solution(mesh):
    spec = P("span", "plane", None)
    return jax.shard_map(
        on_device, mesh=mesh, in_specs=(spec, P()), out_specs=spec, check_vma=False
    )
```

```python
import functools
import math

import jax
import jax.numpy as jnp
import numpy as np
from jax import lax
from jax.experimental import pallas as pl
from jax.experimental.pallas import tpu as pltpu
from jax.sharding import PartitionSpec as P

KMODES = 256
PLANES = 768
STEP = 0.03
VISCOUS = 0.05
STIFF = 4.0

f32 = jnp.float32
bf16 = jnp.bfloat16
NT = (((1,), (1,)), ((), ()))
NN = (((1,), (0,)), ((), ()))
TN = (((0,), (0,)), ((), ()))
VMEM_LIMIT = 56 * 1024 * 1024


def gll_tables():
    x = np.array([-1.0, -math.sqrt(3.0 / 7.0), 0.0, math.sqrt(3.0 / 7.0), 1.0])
    w = np.array([0.1, 49.0 / 90.0, 32.0 / 45.0, 49.0 / 90.0, 0.1])
    q = x * x
    leg = (35.0 * q * q - 30.0 * q + 3.0) / 8.0
    eye = np.eye(5)
    d = np.where(eye > 0, 0.0, leg[:, None] / leg[None, :] / (x[:, None] - x[None, :] + eye))
    d[0, 0], d[4, 4] = -5.0, 5.0
    return d, w, d.T @ (w[:, None] * d)


DIFF, WEIGHT, KMAT = gll_tables()


def halves(table):
    high = table.astype(np.float32).astype(bf16)
    low = (table.astype(np.float32) - high.astype(np.float32)).astype(bf16)
    return high, low


def basis_tables():
    k, p = np.arange(KMODES), np.arange(PLANES)
    angle = 2.0 * math.pi * (p[:, None] * k[None, :] % PLANES) / PLANES
    cos, sin = np.cos(angle), np.sin(angle)
    inverse = np.stack([cos, sin], 2).reshape(PLANES, 2 * KMODES).T / math.sqrt(KMODES)
    factor = np.where(k == 0, 1.0, 2.0) * (math.sqrt(KMODES) / PLANES) * STEP
    ratio = k / KMODES
    inner = np.stack([cos * factor, sin * factor], 2).reshape(PLANES, 2 * KMODES)
    span = np.stack([-ratio * sin * factor, ratio * cos * factor], 2).reshape(PLANES, 2 * KMODES)
    return inverse, inner, span


def split2(x):
    high = x.astype(bf16)
    return high, (x - high.astype(f32)).astype(bf16)


def stack2(x):
    return jnp.concatenate([x, x - x.astype(bf16).astype(f32)], axis=0).astype(bf16)


def dot(a, b, dims=NN):
    return lax.dot_general(a, b, dims, preferred_element_type=f32)


def dot3(stacked, high, low):
    rows = stacked.shape[0] // 2
    both = dot(stacked, high)
    return both[:rows] + both[rows:] + dot(stacked[:rows], low)


def along(mat, a, flip):
    s1, d1, s2, d2, m = a[0] + a[4], a[0] - a[4], a[1] + a[3], a[1] - a[3], a[2]
    out = [None] * 5
    for r in (0, 1):
        e = [0.5 * (mat[r][b] + mat[r][4 - b]) for b in (0, 1)]
        o = [0.5 * (mat[r][b] - mat[r][4 - b]) for b in (0, 1)]
        even = float(e[0]) * s1 + float(e[1]) * s2 + float(mat[r][2]) * m
        odd = float(o[0]) * d1 + float(o[1]) * d2
        out[r] = even + odd
        out[4 - r] = even - odd if flip > 0 else odd - even
    if flip > 0:
        out[2] = float(mat[2][0]) * s1 + float(mat[2][1]) * s2 + float(mat[2][2]) * m
    else:
        out[2] = float(mat[2][0]) * d1 + float(mat[2][1]) * d2
    return out


def two_point10(a, b, qa, qb):
    speed = jnp.maximum(jnp.abs(a), jnp.abs(b))
    return (qa + a * b + qb) * (10.0 / 6.0) - 5.0 * speed * (b - a)


def roll(x, by):
    return pltpu.roll(x, by % x.shape[0], 0)


def pack(x_ref, perm_ref, d_ref, halo_ref, span, chunks, elems):
    rows, modes, cols = x_ref.shape
    block = 5 * elems
    wide = block * chunks
    blocks = span * chunks
    parts = split2(x_ref[...].reshape(rows * modes, cols))
    for s in range(span):
        lo = wide * s // 128 * 128
        hi = -(-wide * (s + 1) // 128) * 128
        perm = perm_ref[s, :, : hi - lo]
        got = sum(dot(perm, part[:, lo:hi], NT) for part in parts)
        for k in range(chunks):
            for j in range(rows):
                d_ref[s * chunks + k, block * j : block * (j + 1), :] = got[
                    block * k : block * (k + 1), modes * j : modes * (j + 1)
                ]
    for s in range(span):
        left = (s * chunks - 1) % blocks
        for j in range(rows):
            last = block * j + block - 1
            halo_ref[s, j : j + 1, :] = d_ref[left, last : last + 1, :]
            for k in range(chunks):
                right = (s * chunks + k + 1) % blocks
                at = rows * (k + 1) + j
                halo_ref[s, at : at + 1, :] = d_ref[right, block * j : block * j + 1, :]
        used = rows * (chunks + 1)
        halo_ref[s, used:, :] = jnp.zeros((halo_ref.shape[1] - used, modes), f32)


def perm_tables(span, chunks, elems):
    wide = 5 * elems * chunks
    width = max(-(-wide * (s + 1) // 128) * 128 - wide * s // 128 * 128 for s in range(span))
    perm = np.zeros((span, wide, width), np.float32)
    for s in range(span):
        lo = wide * s // 128 * 128
        for k in range(chunks):
            for i in range(5):
                for e in range(elems):
                    row = (k * 5 + i) * elems + e
                    perm[s, row, wide * s + 5 * (k * elems + e) + i - lo] = 1.0
    return perm.astype(bf16)


def to_planes(parts, inv_ref, fld_ref, lo):
    x = jnp.concatenate(
        [jnp.concatenate([p[s] for s in range(p.shape[0])], axis=1) for p in parts], axis=0
    )
    stacked = stack2(x)
    for n in range(PLANES // 256):
        at = slice(n * 256, (n + 1) * 256)
        bh, bl = inv_ref[0, :, at], inv_ref[1, :, at]
        fld_ref[lo : lo + x.shape[0], at] = dot3(stacked, bh, bl)


def outer_rows(fld_ref, tag, elems, first, last):
    block = 5 * elems
    sr = 5 * block

    @pl.when(first)
    def _():
        own = fld_ref[0:block, :]
        fld_ref[sr : sr + block, :] = jnp.where(tag == 1, -own, own)

    @pl.when(last)
    def _():
        fld_ref[sr + block : sr + 2 * block, :] = fld_ref[4 * block : 5 * block, :]


def pointwise(fld_ref, halo_ref, edge_ref, carry_ref, r_ref, h_ref, elems, k, chunks):
    block = 5 * elems
    sr = 5 * block
    lane = 128
    place = {0: 0, 4: 4 * elems}
    for j in (1, 2, 3):
        place[j] = 4 * elems * (j + 1) + 8
    third = DIFF * (-1.0 / 3.0)

    def body(n, _):
        at = pl.ds(pl.multiple_of(n * lane, lane), lane)
        row = lax.broadcasted_iota(jnp.int32, (elems, lane), 0)

        def load(base):
            return fld_ref[base : base + elems, at]

        u = [[load(block * j + elems * i) for i in range(5)] for j in range(5)]
        q = [[v * v for v in r] for r in u]
        rhs = [[None] * 5 for _ in range(5)]
        for j in range(5):
            du = along(third, u[j], -1)
            dq = along(third, q[j], -1)
            for i in range(5):
                rhs[j][i] = dq[i] + u[j][i] * du[i]
            hl = halo_ref[j : j + 1, at] if k == 0 else edge_ref[j : j + 1, at]
            hr = halo_ref[5 * (k + 1) + j : 5 * (k + 1) + j + 1, at]
            edge_ref[j : j + 1, at] = u[j][4][elems - 1 : elems, :]
            left = jnp.where(row == 0, hl, roll(u[j][4], 1))
            right = jnp.where(row == elems - 1, hr, roll(u[j][0], -1))
            rhs[j][0] += two_point10(left, u[j][0], left * left, q[j][0]) - 5.0 * q[j][0]
            rhs[j][4] -= two_point10(u[j][4], right, q[j][4], right * right) - 5.0 * q[j][4]
        for i in range(5):
            ui, qi = [u[j][i] for j in range(5)], [q[j][i] for j in range(5)]
            du = along(third, ui, -1)
            dq = along(third, qi, -1)
            for j in range(5):
                rhs[j][i] += dq[j] + ui[j] * du[j]
            lower = load(sr + elems * i)
            upper = load(sr + block + elems * i)
            rhs[0][i] += two_point10(lower, ui[0], lower * lower, qi[0]) - 5.0 * qi[0]
            rhs[4][i] -= two_point10(ui[4], upper, qi[4], upper * upper) - 5.0 * qi[4]
        for ref, val, scale, base in ((r_ref, rhs, None, 0), (h_ref, q, 0.5, 5)):
            for n, j in enumerate((0, 4, 1, 2, 3)):
                a = val[j] if scale is None else [scale * v for v in val[j]]
                kept = 0.0 if k == 0 else carry_ref[base + j : base + j + 1, at]
                ref[place[j] : place[j] + elems, at] = a[0] + jnp.where(
                    row == 0, kept, roll(a[4], 1)
                )
                for i in (1, 2, 3):
                    to = place[j] + elems * i
                    ref[to : to + elems, at] = a[i]
                tail = a[4][elems - 1 : elems, :]
                if k == chunks - 1:
                    ref[8 * elems + n : 8 * elems + n + 1, at] = tail
                else:
                    carry_ref[base + j : base + j + 1, at] = tail
            if k == chunks - 1:
                ref[8 * elems + 5 : 8 * elems + 8, at] = jnp.zeros((3, lane), f32)
            else:
                ref[8 * elems : 8 * elems + 8, at] = jnp.zeros((8, lane), f32)
        return 0

    lax.fori_loop(0, PLANES // lane, body, 0)


def spectral(r_ref, h_ref, fwd_ref, t_ref):
    span, _, modes = t_ref.shape
    rs, hs = stack2(r_ref[...]), stack2(h_ref[...])
    step = max(modes, 256)
    for n in range(span * modes // step):
        at = slice(n * step, (n + 1) * step)
        a, b = fwd_ref[0, :, at], fwd_ref[1, :, at]
        c, d = fwd_ref[2, :, at], fwd_ref[3, :, at]
        t = dot3(rs, a, b) + dot3(hs, c, d)
        for k in range(step // modes):
            s = n * (step // modes) + k
            t_ref[s] = t[:, modes * k : modes * (k + 1)]


def column_load(d_ref, c_ref, elems, js):
    blocks, _, modes = d_ref.shape
    block = 5 * elems
    row = lax.broadcasted_iota(jnp.int32, (elems, modes), 0)
    for j in js:
        for b in range(blocks):
            left = (b - 1) % blocks
            for i in range(4):
                at = block * j + elems * i
                val = d_ref[b, at : at + elems, :]
                if i == 0:
                    at4 = block * j + 4 * elems
                    edge = d_ref[left, at4 + elems - 1 : at4 + elems, :]
                    val += jnp.where(row == 0, edge, roll(d_ref[b, at4 : at4 + elems, :], 1))
                c_ref[j, i, elems * b : elems * (b + 1), :] = val * float(WEIGHT[j] * WEIGHT[i])


def add_tendency(v_ref, t_ref, elems, k, chunks):
    span = t_ref.shape[1]
    for j in range(5):
        base = {0: 0, 4: 4 * elems}.get(j, 4 * elems * (j + 1) + 8)
        for s in range(span):
            at = slice(elems * (s * chunks + k), elems * (s * chunks + k + 1))
            for i in range(4):
                part = t_ref[k, s, base + elems * i : base + elems * (i + 1), :]
                v_ref[j, i, at, :] += part * float(WEIGHT[j] * WEIGHT[i])


def add_ends(v_ref, t_ref, elems, chunks):
    span = t_ref.shape[1]
    for n, j in enumerate((0, 4, 1, 2, 3)):
        for s in range(span):
            end = t_ref[chunks - 1, (s - 1) % span, 8 * elems + n : 8 * elems + n + 1, :]
            at = elems * s * chunks
            v_ref[j, 0, at : at + 1, :] += end * float(WEIGHT[j] * WEIGHT[0])


def fold(x):
    return jnp.sum(x.reshape(x.shape[0] // 8, 8, x.shape[1]), axis=0)


COLW = [2.0 * WEIGHT[0], WEIGHT[1], WEIGHT[2], WEIGHT[3]]


def image(v_ref, out_ref, shift):
    total, modes = v_ref.shape[2:]
    row = lax.broadcasted_iota(jnp.int32, (8, modes), 0)

    def along_row(j, at, after):
        a = [v_ref[j, i, at, :] for i in range(4)]
        a.append(jnp.where(row == 7, after, roll(a[0], -1)))
        return a, along(KMAT * (VISCOUS * WEIGHT[j]), a, 1)

    end = slice(total - 8, total)
    ends = tuple(roll(along_row(j, end, v_ref[j, 0, 0:1, :])[1][4], 1) for j in range(5))

    def body(g, carried):
        before, acc = carried
        at = pl.ds(pl.multiple_of(g * 8, 8), 8)
        after = pl.ds(lax.rem(g * 8 + 8, total), 1)
        vals, kx, tails = [], [], []
        for j in range(5):
            a, k = along_row(j, at, v_ref[j, 0, after, :])
            tail = roll(k[4], 1)
            k[0] = k[0] + jnp.where(row == 0, before[j], tail)
            tails.append(tail)
            vals.append(a)
            kx.append(k)
        for i in range(4):
            col = [vals[j][i] for j in range(5)]
            ky = along(KMAT * (VISCOUS * COLW[i]), col, 1)
            for j in range(5):
                val = kx[j][i] + ky[j] + (shift * float(WEIGHT[j] * COLW[i])) * col[j]
                out_ref[j, i, at, :] = val
                acc = acc + val * col[j]
        return tuple(tails), acc

    return lax.fori_loop(0, total // 8, body, (ends, jnp.zeros((8, modes), f32)))[1]


def join_rows(c_ref, lo, hi, prev, theta, v_ref, js):
    for j in js:
        for i in range(4):
            val = c_ref[j, i]
            if j == 0:
                val = val + lo[i]
            if j == 4:
                val = val + hi[i]
            if prev is not None:
                val = val - theta * prev[j, i]
            v_ref[j, i] = val


def squares(v_ref, first, last, js):
    total = 0.0
    for j in js:
        part = sum(fold(v_ref[j, i] * v_ref[j, i]) for i in range(4))
        if j == 0:
            part = part * jnp.where(first, 1.0, 0.5)
        if j == 4:
            part = part * jnp.where(last, 1.0, 0.5)
        total = total + part
    return total


def solve3(nu, theta):
    a = [[nu[r + c + 1] + theta * nu[r + c] for c in range(3)] for r in range(3)]
    l10, l20 = a[1][0] / a[0][0], a[2][0] / a[0][0]
    d1 = a[1][1] - l10 * a[1][0]
    e = a[2][1] - l20 * a[1][0]
    l21 = e / d1
    d2 = a[2][2] - l20 * a[2][0] - l21 * e
    z0 = nu[0]
    z1 = nu[1] - l10 * z0
    z2 = nu[2] - l20 * z0 - l21 * z1
    y2 = z2 / d2
    y1 = z1 / d1 - l21 * y2
    return z0 / a[0][0] - l10 * y1 - l20 * y2, y1, y2


def unpack(v_ref, exp_ref, out_ref):
    rows, four, total, modes = v_ref.shape
    x = jnp.concatenate([v_ref[j].reshape(four * total, modes) for j in range(rows)], axis=1)
    full = sum(dot(part, exp_ref[...], TN) for part in split2(x))
    out_ref[...] = full.reshape(out_ref.shape)


def expand_table(total):
    out = np.zeros((4 * total, 5 * total), np.float32)
    for e in range(total):
        for i in range(5):
            out[(i % 4) * total + (e + i // 4) % total, 5 * e + i] = 1.0
    return out.astype(bf16)


def segment(
    dims, x_ref, perm_ref, tag_ref, inv_hbm, fwd_hbm, exp_hbm, out_ref,
    inv, fwd, expand, w0, w1, w2, d_ref, dh, recv, hrecv, below, above, fld, halo, edge, carry,
    r_ref, h_ref, tsend, zlo, zhi, tjoin, trecv, c_ref, v0, v1, v2, lo, hi, part, parts,
    table_sem, s1, r1, sh, rh, s2, r2, sz, rz, s3, r3, s6, r6, s4, r4, s5, r5,
):
    span, planes, chunks, elems = dims
    modes, bl = x_ref.shape[1], 5 * elems
    sr, ab = 5 * bl, 8 * elems
    me, mp = lax.axis_index("span"), lax.axis_index("plane")
    first, last = mp == 0, mp == planes - 1
    inner, beyond = mp > 0, mp < planes - 1
    up, down = {"plane": lax.rem(mp + 1, planes)}, {"plane": lax.rem(mp + planes - 1, planes)}

    def remote(src, dst, send, recv_sem, device):
        return pltpu.make_async_remote_copy(
            src_ref=src, dst_ref=dst, send_sem=send, recv_sem=recv_sem,
            device_id=device, device_id_type=pl.DeviceIdType.MESH,
        )

    def peer(d):
        return lax.rem(me + d, span)

    barrier = pltpu.get_barrier_semaphore()
    for axis, here, count in (("span", me, span), ("plane", mp, planes)):
        for d in range(1, count):
            pl.semaphore_signal(
                barrier, inc=1, device_id={axis: lax.rem(here + d, count)},
                device_id_type=pl.DeviceIdType.MESH,
            )
    tables = [
        pltpu.make_async_copy(inv_hbm, inv, table_sem.at[0]),
        pltpu.make_async_copy(fwd_hbm, fwd, table_sem.at[1]),
        pltpu.make_async_copy(exp_hbm, expand, table_sem.at[2]),
    ]
    for copy in tables:
        copy.start()

    def to_peers(start):
        for i in range(span - 1):
            d = 1 + lax.rem(i + lax.rem(mp, 2) * (span // 2 - 1), span - 1)
            start(peer(d), d - 1)

    def state_copy(k, s, n):
        src = d_ref.at[s * chunks + k]
        return remote(src, recv.at[k, me], s1.at[k, n], r1.at[k, n], {"span": s})

    def halo_copy(s, n):
        return remote(dh.at[s], hrecv.at[me], sh.at[n], rh.at[n], {"span": s})

    def row_copies(k):
        a = remote(recv.at[k, :, 4 * bl : 5 * bl, :], below.at[k], s2.at[k, 0], r2.at[k, 0], up)
        b = remote(recv.at[k, :, 0:bl, :], above.at[k], s2.at[k, 1], r2.at[k, 1], down)
        return a, b

    def shared_copies(k):
        src = tsend.at[k, :, 0 : ab + 8, :]
        a = remote(src, zlo.at[k], sz.at[k, 0], rz.at[k, 0], up)
        b = remote(src, zhi.at[k], sz.at[k, 1], rz.at[k, 1], down)
        return a, b

    def inner_copy(k, s, n):
        rows = slice(ab + 8, 20 * elems + 8)
        src, dst = tsend.at[k, s, rows, :], trecv.at[k, me, rows, :]
        return remote(src, dst, s3.at[k, n], r3.at[k, n], {"span": s})

    def outer_copy(k, s, n):
        rows = slice(0, ab + 8 if k == chunks - 1 else ab)
        src, dst = tjoin.at[k, s, rows, :], trecv.at[k, me, rows, :]
        return remote(src, dst, s6.at[k, n], r6.at[k, n], {"span": s})

    def join_copies(n):
        a = remote(c_ref.at[4], lo.at[n], s4.at[n, 0], r4.at[n, 0], up)
        b = remote(c_ref.at[0], hi.at[n], s4.at[n, 1], r4.at[n, 1], down)
        return a, b

    def part_copy(d):
        to = {"plane": lax.rem(mp + d, planes)}
        return remote(part, parts.at[mp], s5.at[d - 1], r5.at[d - 1], to)

    def tags(k):
        total = tag_ref.shape[1]
        element = lax.broadcasted_iota(jnp.int32, (elems, total), 0) + (me * chunks + k) * elems
        lane = lax.broadcasted_iota(jnp.int32, (elems, total), 1)
        column = jnp.sum(jnp.where(element == lane, tag_ref[...], 0), axis=1, keepdims=True)
        return jnp.concatenate([column] * 5, axis=0)

    def start_pair(pair):
        pl.when(beyond)(pair[0].start)
        pl.when(inner)(pair[1].start)

    def wait_sent(pair):
        pl.when(beyond)(pair[0].wait_send)
        pl.when(inner)(pair[1].wait_send)

    def wait_got(pair):
        pl.when(inner)(pair[0].wait_recv)
        pl.when(beyond)(pair[1].wait_recv)

    pack(x_ref, perm_ref, d_ref, dh, span, chunks, elems)
    pl.semaphore_wait(barrier, span + planes - 2)
    to_peers(lambda s, n: state_copy(0, s, n).start())
    to_peers(lambda s, n: halo_copy(s, n).start())
    for k in range(chunks):
        recv[k, me] = d_ref[me * chunks + k]
    hrecv[me] = dh[me]

    @pl.when(first)
    def _():
        below[...] = jnp.zeros_like(below)
        zlo[...] = jnp.zeros_like(zlo)
        lo[...] = jnp.zeros_like(lo)

    @pl.when(last)
    def _():
        above[...] = jnp.zeros_like(above)
        zhi[...] = jnp.zeros_like(zhi)
        hi[...] = jnp.zeros_like(hi)

    column_load(d_ref, c_ref, elems, range(5))
    join_rows(c_ref, None, None, None, None, v0, (1, 2, 3))

    def send_shared(k):
        wait_got(shared_copies(k))
        half = 4 * elems
        row = lax.broadcasted_iota(jnp.int32, (8, modes), 0)
        for s in range(span):
            tjoin[k, s, 0:half] = tsend[k, s, 0:half] + zlo[k, s, half:ab]
            tjoin[k, s, half:ab] = tsend[k, s, half:ab] + zhi[k, s, 0:half]
            if k == chunks - 1:
                ends = tsend[k, s, ab : ab + 8]
                ends = ends + jnp.where(row == 0, zlo[k, s, ab + 1 : ab + 2], 0.0)
                ends = ends + jnp.where(row == 1, zhi[k, s, ab : ab + 1], 0.0)
                tjoin[k, s, ab : ab + 8] = ends
        to_peers(lambda s, n: outer_copy(k, s, n).start())
        rows = slice(0, ab + 8 if k == chunks - 1 else ab)
        trecv[k, me, rows] = tjoin[k, me, rows]

    for k in range(chunks):
        for d in range(1, span):
            state_copy(k, peer(d), d - 1).wait_recv()
        start_pair(row_copies(k))
        if k < chunks - 1:
            to_peers(lambda s, n: state_copy(k + 1, s, n).start())
        else:
            start_pair(join_copies(0))
        if k == 0:
            for copy in tables:
                copy.wait()
        to_planes([recv.at[k]], inv, fld, 0)
        if k == 0:
            for d in range(1, span):
                halo_copy(peer(d), d - 1).wait_recv()
            to_planes([hrecv], inv, halo, 0)
        else:
            send_shared(k - 1)
        wait_got(row_copies(k))
        to_planes([below.at[k], above.at[k]], inv, fld, sr)
        outer_rows(fld, tags(k), elems, first, last)
        pointwise(fld, halo, edge, carry, r_ref, h_ref, elems, k, chunks)

        spectral(r_ref, h_ref, fwd, tsend.at[k])
        start_pair(shared_copies(k))
        to_peers(lambda s, n: inner_copy(k, s, n).start())
        rows = slice(ab + 8, 20 * elems + 8)
        trecv[k, me, rows] = tsend[k, me, rows]
    send_shared(chunks - 1)
    wait_got(join_copies(0))
    join_rows(c_ref, lo.at[0], hi.at[0], None, None, v0, (0, 4))
    wait_sent(join_copies(0))

    for k in range(chunks):
        for d in range(1, span):
            inner_copy(k, peer(d), d - 1).wait_recv()
            outer_copy(k, peer(d), d - 1).wait_recv()
        add_tendency(v0, trecv, elems, k, chunks)
    add_ends(v0, trecv, elems, chunks)

    ids = me * modes + lax.broadcasted_iota(jnp.int32, (1, modes), 1)
    wave = lax.shift_right_logical(ids, 1).astype(f32) / KMODES
    shift = 1.0 + STIFF * wave * wave
    theta = 0.6 + 0.254 * (shift - 1.0)
    sums = []
    prev = None
    for n, (v, w) in enumerate(((v0, w0), (v1, w1), (v2, w2))):
        if n > 0:
            join = functools.partial(join_rows, c_ref, lo.at[n], hi.at[n], prev, theta, v)
            join((1, 2, 3))
            wait_got(join_copies(n))
            join((0, 4))
            wait_sent(join_copies(n))
        curve = image(v, c_ref, shift)
        if n < 2:
            start_pair(join_copies(n + 1))
        sums.append(squares(v, first, last, range(5)))
        sums.append(curve)
        if n < 2:
            unpack(v, expand, w)
        prev = v
    rows = [jnp.sum(t, axis=0, keepdims=True) for t in sums]
    part[...] = jnp.concatenate(rows + [jnp.zeros_like(rows[0])] * 2, axis=0)
    for d in range(1, planes):
        part_copy(d).start()
    parts[mp] = part[...]
    unpack(v2, expand, w2)
    for d in range(1, planes):
        part_copy(d).wait_recv()
    got = jnp.sum(parts[...], axis=0)
    n0, h0, n2, h2, n4, h4 = [got[k : k + 1] for k in range(6)]
    nu = [n0, h0 - theta * n0, n2, h2 - theta * n2, n4, h4 - theta * n4]
    y = solve3(nu, theta)
    y = jnp.concatenate(list(y) + [jnp.zeros_like(y[0])] * 5, axis=0).T
    y0, y1, y2 = y[:, 0:1], y[:, 1:2], y[:, 2:3]
    for j in range(5):
        out_ref[j] = y0 * w0[j] + y1 * w1[j] + y2 * w2[j]
    for d in range(1, span):
        halo_copy(peer(d), d - 1).wait_send()
    for k in range(chunks):
        for d in range(1, span):
            state_copy(k, peer(d), d - 1).wait_send()
            inner_copy(k, peer(d), d - 1).wait_send()
            outer_copy(k, peer(d), d - 1).wait_send()
        wait_sent(row_copies(k))
        wait_sent(shared_copies(k))
    for d in range(1, planes):
        part_copy(d).wait_send()


def shape(*dims):
    return jax.ShapeDtypeStruct(dims, f32)


def on_device(state, wall_tag):
    modes, rows, cols = state.shape
    assert rows == 5
    span, planes = lax.axis_size("span"), lax.axis_size("plane")
    total = cols // 5
    mine = total // span
    chunks = mine // 8
    elems = mine // chunks
    bl = 5 * elems
    sr, tr, shared = 5 * bl, 20 * elems + 8, 8 * elems + 8
    halos = -(-5 * (chunks + 1) // 8) * 8
    inverse, inner, outer = basis_tables()
    inv = jnp.asarray(np.stack(halves(inverse)))
    fwd = jnp.asarray(np.stack(halves(inner) + halves(outer)))
    perm = jnp.asarray(perm_tables(span, chunks, elems))
    expand = jnp.asarray(expand_table(total))
    vmem = pl.BlockSpec(memory_space=pltpu.VMEM)
    hbm = pl.BlockSpec(memory_space=pl.ANY)
    buf = lambda *d: pltpu.VMEM(d, f32)
    dma = lambda *d: pltpu.SemaphoreType.DMA(d)
    joined = buf(5, 4, total, modes)
    halo = buf(3, 4, total, modes)

    out = pl.pallas_call(
        functools.partial(segment, (span, planes, chunks, elems)),
        out_shape=shape(5, modes, cols),
        in_specs=[vmem] * 3 + [hbm] * 3,
        out_specs=vmem,
        scratch_shapes=[
            pltpu.VMEM(inv.shape, bf16),
            pltpu.VMEM(fwd.shape, bf16),
            pltpu.VMEM(expand.shape, bf16),
            buf(5, modes, cols), buf(5, modes, cols), buf(5, modes, cols),
            buf(span * chunks, sr, modes),
            buf(span, halos, modes),
            buf(chunks, span, sr, modes),
            buf(span, halos, modes),
            buf(chunks, span, bl, modes),
            buf(chunks, span, bl, modes),
            buf(sr + 2 * bl, PLANES),
            buf(halos, PLANES),
            buf(8, PLANES),
            buf(16, PLANES),
            buf(tr, PLANES),
            buf(tr, PLANES),
            buf(chunks, span, tr, modes),
            buf(chunks, span, shared, modes),
            buf(chunks, span, shared, modes),
            buf(chunks, span, shared, modes),
            buf(chunks, span, tr, modes),
            joined, joined, joined, joined, halo, halo,
            buf(8, modes),
            buf(planes, 8, modes),
            dma(3),
            dma(chunks, span - 1), dma(chunks, span - 1),
            dma(span - 1), dma(span - 1),
            dma(chunks, 2), dma(chunks, 2),
            dma(chunks, 2), dma(chunks, 2),
            dma(chunks, span - 1), dma(chunks, span - 1),
            dma(chunks, span - 1), dma(chunks, span - 1),
            dma(3, 2), dma(3, 2),
            dma(planes - 1), dma(planes - 1),
        ],
        compiler_params=pltpu.CompilerParams(
            vmem_limit_bytes=VMEM_LIMIT, collective_id=0, has_side_effects=True
        ),
    )(state.transpose(1, 0, 2), perm, wall_tag.reshape(1, total), inv, fwd, expand)
    return out.transpose(1, 0, 2)


def solution(mesh):
    spec = P("span", "plane", None)
    return jax.shard_map(
        on_device, mesh=mesh, in_specs=(spec, P()), out_specs=spec, check_vma=False
    )
```

```python
import functools
import math

import jax
import jax.numpy as jnp
import numpy as np
from jax import lax
from jax.experimental import pallas as pl
from jax.experimental.pallas import tpu as pltpu
from jax.sharding import PartitionSpec as P

KMODES = 256
PLANES = 768
STEP = 0.03
VISCOUS = 0.05
STIFF = 4.0

f32 = jnp.float32
bf16 = jnp.bfloat16
NT = (((1,), (1,)), ((), ()))
NN = (((1,), (0,)), ((), ()))
TN = (((0,), (0,)), ((), ()))
VMEM_LIMIT = 56 * 1024 * 1024


def gll_tables():
    x = np.array([-1.0, -math.sqrt(3.0 / 7.0), 0.0, math.sqrt(3.0 / 7.0), 1.0])
    w = np.array([0.1, 49.0 / 90.0, 32.0 / 45.0, 49.0 / 90.0, 0.1])
    q = x * x
    leg = (35.0 * q * q - 30.0 * q + 3.0) / 8.0
    eye = np.eye(5)
    d = np.where(eye > 0, 0.0, leg[:, None] / leg[None, :] / (x[:, None] - x[None, :] + eye))
    d[0, 0], d[4, 4] = -5.0, 5.0
    return d, w, d.T @ (w[:, None] * d)


DIFF, WEIGHT, KMAT = gll_tables()


def halves(table):
    high = table.astype(np.float32).astype(bf16)
    low = (table.astype(np.float32) - high.astype(np.float32)).astype(bf16)
    return high, low


def basis_tables():
    k, p = np.arange(KMODES), np.arange(PLANES)
    angle = 2.0 * math.pi * (p[:, None] * k[None, :] % PLANES) / PLANES
    cos, sin = np.cos(angle), np.sin(angle)
    inverse = np.stack([cos, sin], 2).reshape(PLANES, 2 * KMODES).T / math.sqrt(KMODES)
    factor = np.where(k == 0, 1.0, 2.0) * (math.sqrt(KMODES) / PLANES) * STEP
    ratio = k / KMODES
    inner = np.stack([cos * factor, sin * factor], 2).reshape(PLANES, 2 * KMODES)
    span = np.stack([-ratio * sin * factor, ratio * cos * factor], 2).reshape(PLANES, 2 * KMODES)
    return inverse, inner, span


def split2(x):
    high = x.astype(bf16)
    return high, (x - high.astype(f32)).astype(bf16)


def stack2(x):
    return jnp.concatenate([x, x - x.astype(bf16).astype(f32)], axis=0).astype(bf16)


def dot(a, b, dims=NN):
    return lax.dot_general(a, b, dims, preferred_element_type=f32)


def dot3(stacked, high, low):
    rows = stacked.shape[0] // 2
    both = dot(stacked, high)
    return both[:rows] + both[rows:] + dot(stacked[:rows], low)


def along(mat, a, flip):
    s1, d1, s2, d2, m = a[0] + a[4], a[0] - a[4], a[1] + a[3], a[1] - a[3], a[2]
    out = [None] * 5
    for r in (0, 1):
        e = [0.5 * (mat[r][b] + mat[r][4 - b]) for b in (0, 1)]
        o = [0.5 * (mat[r][b] - mat[r][4 - b]) for b in (0, 1)]
        even = float(e[0]) * s1 + float(e[1]) * s2 + float(mat[r][2]) * m
        odd = float(o[0]) * d1 + float(o[1]) * d2
        out[r] = even + odd
        out[4 - r] = even - odd if flip > 0 else odd - even
    if flip > 0:
        out[2] = float(mat[2][0]) * s1 + float(mat[2][1]) * s2 + float(mat[2][2]) * m
    else:
        out[2] = float(mat[2][0]) * d1 + float(mat[2][1]) * d2
    return out


def two_point10(a, b, qa, qb):
    speed = jnp.maximum(jnp.abs(a), jnp.abs(b))
    return (qa + a * b + qb) * (10.0 / 6.0) - 5.0 * speed * (b - a)


def roll(x, by):
    return pltpu.roll(x, by % x.shape[0], 0)


def pack(x_ref, perm_ref, d_ref, halo_ref, span, chunks, elems):
    rows, modes, cols = x_ref.shape
    block = 5 * elems
    wide = block * chunks
    blocks = span * chunks
    parts = split2(x_ref[...].reshape(rows * modes, cols))
    for s in range(span):
        lo = wide * s // 128 * 128
        hi = -(-wide * (s + 1) // 128) * 128
        perm = perm_ref[s, :, : hi - lo]
        got = sum(dot(perm, part[:, lo:hi], NT) for part in parts)
        for k in range(chunks):
            for j in range(rows):
                d_ref[s * chunks + k, block * j : block * (j + 1), :] = got[
                    block * k : block * (k + 1), modes * j : modes * (j + 1)
                ]
    for s in range(span):
        left = (s * chunks - 1) % blocks
        for j in range(rows):
            last = block * j + block - 1
            halo_ref[s, j : j + 1, :] = d_ref[left, last : last + 1, :]
            for k in range(chunks):
                right = (s * chunks + k + 1) % blocks
                at = rows * (k + 1) + j
                halo_ref[s, at : at + 1, :] = d_ref[right, block * j : block * j + 1, :]
        used = rows * (chunks + 1)
        halo_ref[s, used:, :] = jnp.zeros((halo_ref.shape[1] - used, modes), f32)


def perm_tables(span, chunks, elems):
    wide = 5 * elems * chunks
    width = max(-(-wide * (s + 1) // 128) * 128 - wide * s // 128 * 128 for s in range(span))
    perm = np.zeros((span, wide, width), np.float32)
    for s in range(span):
        lo = wide * s // 128 * 128
        for k in range(chunks):
            for i in range(5):
                for e in range(elems):
                    row = (k * 5 + i) * elems + e
                    perm[s, row, wide * s + 5 * (k * elems + e) + i - lo] = 1.0
    return perm.astype(bf16)


def to_planes(parts, inv_ref, fld_ref, lo):
    x = jnp.concatenate(
        [jnp.concatenate([p[s] for s in range(p.shape[0])], axis=1) for p in parts], axis=0
    )
    stacked = stack2(x)
    for n in range(PLANES // 256):
        at = slice(n * 256, (n + 1) * 256)
        bh, bl = inv_ref[0, :, at], inv_ref[1, :, at]
        fld_ref[lo : lo + x.shape[0], at] = dot3(stacked, bh, bl)


def outer_rows(fld_ref, tag, elems, first, last):
    block = 5 * elems
    sr = 5 * block

    @pl.when(first)
    def _():
        own = fld_ref[0:block, :]
        fld_ref[sr : sr + block, :] = jnp.where(tag == 1, -own, own)

    @pl.when(last)
    def _():
        fld_ref[sr + block : sr + 2 * block, :] = fld_ref[4 * block : 5 * block, :]


def pointwise(fld_ref, halo_ref, edge_ref, carry_ref, r_ref, h_ref, elems, k, chunks):
    block = 5 * elems
    sr = 5 * block
    lane = 128
    place = {0: 0, 4: 4 * elems + 8}
    for j in (1, 2, 3):
        place[j] = 4 * elems * (j + 1) + 8
    third = DIFF * (-1.0 / 3.0)

    def body(n, _):
        at = pl.ds(pl.multiple_of(n * lane, lane), lane)
        row = lax.broadcasted_iota(jnp.int32, (elems, lane), 0)

        def load(base):
            return fld_ref[base : base + elems, at]

        u = [[load(block * j + elems * i) for i in range(5)] for j in range(5)]
        q = [[v * v for v in r] for r in u]
        rhs = [[None] * 5 for _ in range(5)]
        for j in range(5):
            du = along(third, u[j], -1)
            dq = along(third, q[j], -1)
            for i in range(5):
                rhs[j][i] = dq[i] + u[j][i] * du[i]
            hl = halo_ref[j : j + 1, at] if k == 0 else edge_ref[j : j + 1, at]
            hr = halo_ref[5 * (k + 1) + j : 5 * (k + 1) + j + 1, at]
            edge_ref[j : j + 1, at] = u[j][4][elems - 1 : elems, :]
            left = jnp.where(row == 0, hl, roll(u[j][4], 1))
            right = jnp.where(row == elems - 1, hr, roll(u[j][0], -1))
            rhs[j][0] += two_point10(left, u[j][0], left * left, q[j][0]) - 5.0 * q[j][0]
            rhs[j][4] -= two_point10(u[j][4], right, q[j][4], right * right) - 5.0 * q[j][4]
        for i in range(5):
            ui, qi = [u[j][i] for j in range(5)], [q[j][i] for j in range(5)]
            du = along(third, ui, -1)
            dq = along(third, qi, -1)
            for j in range(5):
                rhs[j][i] += dq[j] + ui[j] * du[j]
            lower = load(sr + elems * i)
            upper = load(sr + block + elems * i)
            rhs[0][i] += two_point10(lower, ui[0], lower * lower, qi[0]) - 5.0 * qi[0]
            rhs[4][i] -= two_point10(ui[4], upper, qi[4], upper * upper) - 5.0 * qi[4]
        for ref, val, scale, base in ((r_ref, rhs, None, 0), (h_ref, q, 0.5, 5)):
            for n, j in enumerate((0, 4, 1, 2, 3)):
                a = val[j] if scale is None else [scale * v for v in val[j]]
                kept = 0.0 if k == 0 else carry_ref[base + j : base + j + 1, at]
                ref[place[j] : place[j] + elems, at] = a[0] + jnp.where(
                    row == 0, kept, roll(a[4], 1)
                )
                for i in (1, 2, 3):
                    to = place[j] + elems * i
                    ref[to : to + elems, at] = a[i]
                tail = a[4][elems - 1 : elems, :]
                if k == chunks - 1:
                    ref[4 * elems + n : 4 * elems + n + 1, at] = tail
                else:
                    carry_ref[base + j : base + j + 1, at] = tail
            if k == chunks - 1:
                ref[4 * elems + 5 : 4 * elems + 8, at] = jnp.zeros((3, lane), f32)
            else:
                ref[4 * elems : 4 * elems + 8, at] = jnp.zeros((8, lane), f32)
        return 0

    lax.fori_loop(0, PLANES // lane, body, 0)


def spectral(r_ref, h_ref, fwd_ref, t_ref):
    span, _, modes = t_ref.shape
    rs, hs = stack2(r_ref[...]), stack2(h_ref[...])
    step = max(modes, 256)
    for n in range(span * modes // step):
        at = slice(n * step, (n + 1) * step)
        a, b = fwd_ref[0, :, at], fwd_ref[1, :, at]
        c, d = fwd_ref[2, :, at], fwd_ref[3, :, at]
        t = dot3(rs, a, b) + dot3(hs, c, d)
        for k in range(step // modes):
            s = n * (step // modes) + k
            t_ref[s] = t[:, modes * k : modes * (k + 1)]


def column_load(d_ref, c_ref, elems, js):
    blocks, _, modes = d_ref.shape
    block = 5 * elems
    row = lax.broadcasted_iota(jnp.int32, (elems, modes), 0)
    for j in js:
        for b in range(blocks):
            left = (b - 1) % blocks
            for i in range(4):
                at = block * j + elems * i
                val = d_ref[b, at : at + elems, :]
                if i == 0:
                    at4 = block * j + 4 * elems
                    edge = d_ref[left, at4 + elems - 1 : at4 + elems, :]
                    val += jnp.where(row == 0, edge, roll(d_ref[b, at4 : at4 + elems, :], 1))
                c_ref[j, i, elems * b : elems * (b + 1), :] = val * float(WEIGHT[j] * WEIGHT[i])


def add_tendency(v_ref, t_ref, elems, k, chunks):
    span = t_ref.shape[1]
    for j in range(5):
        base = {0: 0, 4: 4 * elems + 8}.get(j, 4 * elems * (j + 1) + 8)
        for s in range(span):
            at = slice(elems * (s * chunks + k), elems * (s * chunks + k + 1))
            for i in range(4):
                part = t_ref[k, s, base + elems * i : base + elems * (i + 1), :]
                v_ref[j, i, at, :] += part * float(WEIGHT[j] * WEIGHT[i])


def add_ends(v_ref, t_ref, elems, chunks):
    span = t_ref.shape[1]
    for n, j in enumerate((0, 4, 1, 2, 3)):
        for s in range(span):
            end = t_ref[chunks - 1, (s - 1) % span, 4 * elems + n : 4 * elems + n + 1, :]
            at = elems * s * chunks
            v_ref[j, 0, at : at + 1, :] += end * float(WEIGHT[j] * WEIGHT[0])


def fold(x):
    return jnp.sum(x.reshape(x.shape[0] // 8, 8, x.shape[1]), axis=0)


COLW = [2.0 * WEIGHT[0], WEIGHT[1], WEIGHT[2], WEIGHT[3]]


def image(v_ref, out_ref, shift):
    total, modes = v_ref.shape[2:]
    row = lax.broadcasted_iota(jnp.int32, (8, modes), 0)

    def along_row(j, at, after):
        a = [v_ref[j, i, at, :] for i in range(4)]
        a.append(jnp.where(row == 7, after, roll(a[0], -1)))
        return a, along(KMAT * (VISCOUS * WEIGHT[j]), a, 1)

    end = slice(total - 8, total)
    ends = tuple(roll(along_row(j, end, v_ref[j, 0, 0:1, :])[1][4], 1) for j in range(5))

    def body(g, carried):
        before, acc = carried
        at = pl.ds(pl.multiple_of(g * 8, 8), 8)
        after = pl.ds(lax.rem(g * 8 + 8, total), 1)
        vals, kx, tails = [], [], []
        for j in range(5):
            a, k = along_row(j, at, v_ref[j, 0, after, :])
            tail = roll(k[4], 1)
            k[0] = k[0] + jnp.where(row == 0, before[j], tail)
            tails.append(tail)
            vals.append(a)
            kx.append(k)
        for i in range(4):
            col = [vals[j][i] for j in range(5)]
            ky = along(KMAT * (VISCOUS * COLW[i]), col, 1)
            for j in range(5):
                val = kx[j][i] + ky[j] + (shift * float(WEIGHT[j] * COLW[i])) * col[j]
                out_ref[j, i, at, :] = val
                acc = acc + val * col[j]
        return tuple(tails), acc

    return lax.fori_loop(0, total // 8, body, (ends, jnp.zeros((8, modes), f32)))[1]


def join_rows(c_ref, lo, hi, prev, theta, v_ref, js):
    for j in js:
        for i in range(4):
            val = c_ref[j, i]
            if j == 0:
                val = val + lo[i]
            if j == 4:
                val = val + hi[i]
            if prev is not None:
                val = val - theta * prev[j, i]
            v_ref[j, i] = val


def squares(v_ref, first, last, js):
    total = 0.0
    for j in js:
        part = sum(fold(v_ref[j, i] * v_ref[j, i]) for i in range(4))
        if j == 0:
            part = part * jnp.where(first, 1.0, 0.5)
        if j == 4:
            part = part * jnp.where(last, 1.0, 0.5)
        total = total + part
    return total


def solve3(nu, theta):
    a = [[nu[r + c + 1] + theta * nu[r + c] for c in range(3)] for r in range(3)]
    l10, l20 = a[1][0] / a[0][0], a[2][0] / a[0][0]
    d1 = a[1][1] - l10 * a[1][0]
    e = a[2][1] - l20 * a[1][0]
    l21 = e / d1
    d2 = a[2][2] - l20 * a[2][0] - l21 * e
    z0 = nu[0]
    z1 = nu[1] - l10 * z0
    z2 = nu[2] - l20 * z0 - l21 * z1
    y2 = z2 / d2
    y1 = z1 / d1 - l21 * y2
    return z0 / a[0][0] - l10 * y1 - l20 * y2, y1, y2


def unpack(v_ref, exp_ref, out_ref):
    rows, four, total, modes = v_ref.shape
    x = jnp.concatenate([v_ref[j].reshape(four * total, modes) for j in range(rows)], axis=1)
    full = sum(dot(part, exp_ref[...], TN) for part in split2(x))
    out_ref[...] = full.reshape(out_ref.shape)


def expand_table(total):
    out = np.zeros((4 * total, 5 * total), np.float32)
    for e in range(total):
        for i in range(5):
            out[(i % 4) * total + (e + i // 4) % total, 5 * e + i] = 1.0
    return out.astype(bf16)


def segment(
    dims, x_ref, perm_ref, tag_ref, inv_hbm, fwd_hbm, exp_hbm, out_ref,
    inv, fwd, expand, w0, w1, w2, d_ref, dh, recv, hrecv, below, above, fld, halo, edge, carry,
    r_ref, h_ref, tsend, zlo, zhi, tjoin, trecv, c_ref, v0, v1, v2, lo, hi, part, parts,
    table_sem, s1, r1, sh, rh, s2, r2, sz, rz, s3, r3, s6, r6, s4, r4, s5, r5,
):
    span, planes, chunks, elems = dims
    modes, bl = x_ref.shape[1], 5 * elems
    sr, ab = 5 * bl, 8 * elems
    me, mp = lax.axis_index("span"), lax.axis_index("plane")
    first, last = mp == 0, mp == planes - 1
    inner, beyond = mp > 0, mp < planes - 1
    up, down = {"plane": lax.rem(mp + 1, planes)}, {"plane": lax.rem(mp + planes - 1, planes)}

    def remote(src, dst, send, recv_sem, device):
        return pltpu.make_async_remote_copy(
            src_ref=src, dst_ref=dst, send_sem=send, recv_sem=recv_sem,
            device_id=device, device_id_type=pl.DeviceIdType.MESH,
        )

    def peer(d):
        return lax.rem(me + d, span)

    barrier = pltpu.get_barrier_semaphore()
    for axis, here, count in (("span", me, span), ("plane", mp, planes)):
        for d in range(1, count):
            pl.semaphore_signal(
                barrier, inc=1, device_id={axis: lax.rem(here + d, count)},
                device_id_type=pl.DeviceIdType.MESH,
            )
    tables = [
        pltpu.make_async_copy(inv_hbm, inv, table_sem.at[0]),
        pltpu.make_async_copy(fwd_hbm, fwd, table_sem.at[1]),
        pltpu.make_async_copy(exp_hbm, expand, table_sem.at[2]),
    ]
    for copy in tables:
        copy.start()

    def to_peers(start):
        for i in range(span - 1):
            d = 1 + lax.rem(i + lax.rem(mp, 2) * (span // 2 - 1), span - 1)
            start(peer(d), d - 1)

    def state_copy(k, s, n):
        src = d_ref.at[s * chunks + k]
        return remote(src, recv.at[k, me], s1.at[k, n], r1.at[k, n], {"span": s})

    def halo_copy(s, n):
        return remote(dh.at[s], hrecv.at[me], sh.at[n], rh.at[n], {"span": s})

    def row_copies(k):
        a = remote(recv.at[k, :, 4 * bl : 5 * bl, :], below.at[k], s2.at[k, 0], r2.at[k, 0], up)
        b = remote(recv.at[k, :, 0:bl, :], above.at[k], s2.at[k, 1], r2.at[k, 1], down)
        return a, b

    def shared_copies(k):
        top, low = slice(4 * elems, ab + 8), slice(0, 4 * elems + 8)
        a = remote(tsend.at[k, :, top, :], zlo.at[k], sz.at[k, 0], rz.at[k, 0], up)
        b = remote(tsend.at[k, :, low, :], zhi.at[k], sz.at[k, 1], rz.at[k, 1], down)
        return a, b

    def inner_copy(k, s, n):
        rows = slice(ab + 8, 20 * elems + 8)
        src, dst = tsend.at[k, s, rows, :], trecv.at[k, me, rows, :]
        return remote(src, dst, s3.at[k, n], r3.at[k, n], {"span": s})

    def outer_copy(k, s, n):
        rows = slice(0, ab + 8)
        src, dst = tjoin.at[k, s, rows, :], trecv.at[k, me, rows, :]
        return remote(src, dst, s6.at[k, n], r6.at[k, n], {"span": s})

    def join_copies(n):
        a = remote(c_ref.at[4], lo.at[n], s4.at[n, 0], r4.at[n, 0], up)
        b = remote(c_ref.at[0], hi.at[n], s4.at[n, 1], r4.at[n, 1], down)
        return a, b

    def part_copy(d):
        to = {"plane": lax.rem(mp + d, planes)}
        return remote(part, parts.at[mp], s5.at[d - 1], r5.at[d - 1], to)

    def tags(k):
        total = tag_ref.shape[1]
        element = lax.broadcasted_iota(jnp.int32, (elems, total), 0) + (me * chunks + k) * elems
        lane = lax.broadcasted_iota(jnp.int32, (elems, total), 1)
        column = jnp.sum(jnp.where(element == lane, tag_ref[...], 0), axis=1, keepdims=True)
        return jnp.concatenate([column] * 5, axis=0)

    def start_pair(pair):
        pl.when(beyond)(pair[0].start)
        pl.when(inner)(pair[1].start)

    def wait_sent(pair):
        pl.when(beyond)(pair[0].wait_send)
        pl.when(inner)(pair[1].wait_send)

    def wait_got(pair):
        pl.when(inner)(pair[0].wait_recv)
        pl.when(beyond)(pair[1].wait_recv)

    pack(x_ref, perm_ref, d_ref, dh, span, chunks, elems)
    pl.semaphore_wait(barrier, span + planes - 2)
    to_peers(lambda s, n: state_copy(0, s, n).start())
    to_peers(lambda s, n: halo_copy(s, n).start())
    for k in range(chunks):
        recv[k, me] = d_ref[me * chunks + k]
    hrecv[me] = dh[me]

    @pl.when(first)
    def _():
        below[...] = jnp.zeros_like(below)
        zlo[...] = jnp.zeros_like(zlo)
        lo[...] = jnp.zeros_like(lo)

    @pl.when(last)
    def _():
        above[...] = jnp.zeros_like(above)
        zhi[...] = jnp.zeros_like(zhi)
        hi[...] = jnp.zeros_like(hi)

    column_load(d_ref, c_ref, elems, range(5))
    join_rows(c_ref, None, None, None, None, v0, (1, 2, 3))

    def send_shared(k):
        wait_got(shared_copies(k))
        half = 4 * elems
        row = lax.broadcasted_iota(jnp.int32, (8, modes), 0)
        for s in range(span):
            tjoin[k, s, 0:half] = tsend[k, s, 0:half] + zlo[k, s, 8 : half + 8]
            tjoin[k, s, half + 8 :] = tsend[k, s, half + 8 : ab + 8] + zhi[k, s, 0:half]
            ends = tsend[k, s, half : half + 8]
            if k == chunks - 1:
                ends = ends + jnp.where(row == 0, zlo[k, s, 1:2], 0.0)
                ends = ends + jnp.where(row == 1, zhi[k, s, half : half + 1], 0.0)
            tjoin[k, s, half : half + 8] = ends
        to_peers(lambda s, n: outer_copy(k, s, n).start())
        rows = slice(0, ab + 8)
        trecv[k, me, rows] = tjoin[k, me, rows]

    for k in range(chunks):
        for d in range(1, span):
            state_copy(k, peer(d), d - 1).wait_recv()
        start_pair(row_copies(k))
        if k < chunks - 1:
            to_peers(lambda s, n: state_copy(k + 1, s, n).start())
        else:
            start_pair(join_copies(0))
        if k == 0:
            for copy in tables:
                copy.wait()
        to_planes([recv.at[k]], inv, fld, 0)
        if k == 0:
            for d in range(1, span):
                halo_copy(peer(d), d - 1).wait_recv()
            to_planes([hrecv], inv, halo, 0)
        else:
            send_shared(k - 1)
        wait_got(row_copies(k))
        to_planes([below.at[k], above.at[k]], inv, fld, sr)
        outer_rows(fld, tags(k), elems, first, last)
        pointwise(fld, halo, edge, carry, r_ref, h_ref, elems, k, chunks)

        spectral(r_ref, h_ref, fwd, tsend.at[k])
        start_pair(shared_copies(k))
        to_peers(lambda s, n: inner_copy(k, s, n).start())
        rows = slice(ab + 8, 20 * elems + 8)
        trecv[k, me, rows] = tsend[k, me, rows]
    send_shared(chunks - 1)
    wait_got(join_copies(0))
    join_rows(c_ref, lo.at[0], hi.at[0], None, None, v0, (0, 4))
    wait_sent(join_copies(0))

    for k in range(chunks):
        for d in range(1, span):
            inner_copy(k, peer(d), d - 1).wait_recv()
            outer_copy(k, peer(d), d - 1).wait_recv()
        add_tendency(v0, trecv, elems, k, chunks)
    add_ends(v0, trecv, elems, chunks)

    ids = me * modes + lax.broadcasted_iota(jnp.int32, (1, modes), 1)
    wave = lax.shift_right_logical(ids, 1).astype(f32) / KMODES
    shift = 1.0 + STIFF * wave * wave
    theta = 0.6 + 0.254 * (shift - 1.0)
    sums = []
    prev = None
    for n, (v, w) in enumerate(((v0, w0), (v1, w1), (v2, w2))):
        if n > 0:
            join = functools.partial(join_rows, c_ref, lo.at[n], hi.at[n], prev, theta, v)
            join((1, 2, 3))
            wait_got(join_copies(n))
            join((0, 4))
            wait_sent(join_copies(n))
        curve = image(v, c_ref, shift)
        if n < 2:
            start_pair(join_copies(n + 1))
        sums.append(squares(v, first, last, range(5)))
        sums.append(curve)
        if n < 2:
            unpack(v, expand, w)
        prev = v
    rows = [jnp.sum(t, axis=0, keepdims=True) for t in sums]
    part[...] = jnp.concatenate(rows + [jnp.zeros_like(rows[0])] * 2, axis=0)
    for d in range(1, planes):
        part_copy(d).start()
    parts[mp] = part[...]
    unpack(v2, expand, w2)
    for d in range(1, planes):
        part_copy(d).wait_recv()
    got = jnp.sum(parts[...], axis=0)
    n0, h0, n2, h2, n4, h4 = [got[k : k + 1] for k in range(6)]
    nu = [n0, h0 - theta * n0, n2, h2 - theta * n2, n4, h4 - theta * n4]
    y = solve3(nu, theta)
    y = jnp.concatenate(list(y) + [jnp.zeros_like(y[0])] * 5, axis=0).T
    y0, y1, y2 = y[:, 0:1], y[:, 1:2], y[:, 2:3]
    for j in range(5):
        out_ref[j] = y0 * w0[j] + y1 * w1[j] + y2 * w2[j]
    for d in range(1, span):
        halo_copy(peer(d), d - 1).wait_send()
    for k in range(chunks):
        for d in range(1, span):
            state_copy(k, peer(d), d - 1).wait_send()
            inner_copy(k, peer(d), d - 1).wait_send()
            outer_copy(k, peer(d), d - 1).wait_send()
        wait_sent(row_copies(k))
        wait_sent(shared_copies(k))
    for d in range(1, planes):
        part_copy(d).wait_send()


def shape(*dims):
    return jax.ShapeDtypeStruct(dims, f32)


def on_device(state, wall_tag):
    modes, rows, cols = state.shape
    assert rows == 5
    span, planes = lax.axis_size("span"), lax.axis_size("plane")
    total = cols // 5
    mine = total // span
    chunks = mine // 8
    elems = mine // chunks
    bl = 5 * elems
    sr, tr, shared = 5 * bl, 20 * elems + 8, 8 * elems + 8
    halos = -(-5 * (chunks + 1) // 8) * 8
    inverse, inner, outer = basis_tables()
    inv = jnp.asarray(np.stack(halves(inverse)))
    fwd = jnp.asarray(np.stack(halves(inner) + halves(outer)))
    perm = jnp.asarray(perm_tables(span, chunks, elems))
    expand = jnp.asarray(expand_table(total))
    vmem = pl.BlockSpec(memory_space=pltpu.VMEM)
    hbm = pl.BlockSpec(memory_space=pl.ANY)
    buf = lambda *d: pltpu.VMEM(d, f32)
    dma = lambda *d: pltpu.SemaphoreType.DMA(d)
    joined = buf(5, 4, total, modes)
    halo = buf(3, 4, total, modes)

    out = pl.pallas_call(
        functools.partial(segment, (span, planes, chunks, elems)),
        out_shape=shape(5, modes, cols),
        in_specs=[vmem] * 3 + [hbm] * 3,
        out_specs=vmem,
        scratch_shapes=[
            pltpu.VMEM(inv.shape, bf16),
            pltpu.VMEM(fwd.shape, bf16),
            pltpu.VMEM(expand.shape, bf16),
            buf(5, modes, cols), buf(5, modes, cols), buf(5, modes, cols),
            buf(span * chunks, sr, modes),
            buf(span, halos, modes),
            buf(chunks, span, sr, modes),
            buf(span, halos, modes),
            buf(chunks, span, bl, modes),
            buf(chunks, span, bl, modes),
            buf(sr + 2 * bl, PLANES),
            buf(halos, PLANES),
            buf(8, PLANES),
            buf(16, PLANES),
            buf(tr, PLANES),
            buf(tr, PLANES),
            buf(chunks, span, tr, modes),
            buf(chunks, span, 4 * elems + 8, modes),
            buf(chunks, span, 4 * elems + 8, modes),
            buf(chunks, span, shared, modes),
            buf(chunks, span, tr, modes),
            joined, joined, joined, joined, halo, halo,
            buf(8, modes),
            buf(planes, 8, modes),
            dma(3),
            dma(chunks, span - 1), dma(chunks, span - 1),
            dma(span - 1), dma(span - 1),
            dma(chunks, 2), dma(chunks, 2),
            dma(chunks, 2), dma(chunks, 2),
            dma(chunks, span - 1), dma(chunks, span - 1),
            dma(chunks, span - 1), dma(chunks, span - 1),
            dma(3, 2), dma(3, 2),
            dma(planes - 1), dma(planes - 1),
        ],
        compiler_params=pltpu.CompilerParams(
            vmem_limit_bytes=VMEM_LIMIT, collective_id=0, has_side_effects=True
        ),
    )(state.transpose(1, 0, 2), perm, wall_tag.reshape(1, total), inv, fwd, expand)
    return out.transpose(1, 0, 2)


def solution(mesh):
    spec = P("span", "plane", None)
    return jax.shard_map(
        on_device, mesh=mesh, in_specs=(spec, P()), out_specs=spec, check_vma=False
    )
```
